32 devices in a mesh: row: 16 (over z, y, x), col: 2 (over core).
Axes of the slice: x: 2, y: 2, z: 4, core: 2. Of those that a mesh axis runs over, the one named last changes fastest.
Arguments:
- object_field: float32 [2, 4096, 512], P(None, 'row', 'col'), may hold values from -6 to 6
- probe_field: float32 [2, 256, 256], replicated, may hold values from -6 to 6
- amplitudes: float32 [32, 512, 256], P('row', 'col'), may hold values from 0 to 4
- offsets: int32 [16, 2, 2, 2], P('row', 'col'), may hold values from 0 to 128, as said below
- counts: int32 [16, 2], P('row', 'col'), may hold values from 1 to 2
Outputs:
- object_out: float32 [2, 4096, 512], P(None, 'row', 'col')
- probe_out: float32 [2, 256, 256], replicated
The draws below stay inside these ranges and needn't reach their ends.
Inputs may be any that keep to these rules, and one draw needn't show every extreme that they name: `offsets`: slots from counts[r, c] on are padding and hold no window.
All inputs are finite; a program needn't handle non-finite values.
Results may differ from the reference program's by a relative error of at most 0.0003.
Values sent between devices are 32-bit elements; how exact they have to be, the bound alone decides.
A program may use at most 64 MiB of HBM per device.

```python
import jax
import jax.numpy as jnp
from jax import lax

WIN = 256
TILE = 256
HALO = 128
MOST = 2
OUTER = 2
INNER = 1
TILES_DOWN = 16
TILES_ACROSS = 2
OBJ_ROWS = 4096
OBJ_COLS = 512


def draw_counts(key, part):
    tiles_down = OBJ_ROWS // TILE
    tiles_across = OBJ_COLS // TILE
    key_heavy = jax.random.fold_in(key, 11)
    key_light = jax.random.fold_in(key, 12)
    key_rowpick = jax.random.fold_in(key, 13)
    key_colpick = jax.random.fold_in(key, 14)
    heavy_pick = jax.random.randint(key_heavy, (tiles_down, tiles_across), 0, 4)
    lighter = jax.random.randint(key_light, (tiles_down, tiles_across), 1, MOST // 2 + 2)
    lighter = jnp.minimum(lighter, MOST)
    counted = jnp.where(heavy_pick == 0, MOST, lighter).astype(jnp.int32)
    row_spot = jax.random.randint(key_rowpick, (), 0, tiles_down)
    col_spot = jax.random.randint(key_colpick, (), 0, tiles_across)
    return counted.at[row_spot, col_spot].set(MOST).astype(jnp.int32)


def draw_offsets(key, part):
    tiles_down = OBJ_ROWS // TILE
    tiles_across = OBJ_COLS // TILE
    key_values = jax.random.fold_in(key, 21)
    key_rowpick = jax.random.fold_in(key, 22)
    key_colpick = jax.random.fold_in(key, 23)
    drawn = jax.random.randint(key_values, (tiles_down, tiles_across, MOST, 2), 0, HALO + 1)
    row_spot = jax.random.randint(key_rowpick, (), 0, tiles_down)
    col_spot = jax.random.randint(key_colpick, (), 0, tiles_across)
    other_row = (row_spot + 1) % tiles_down
    drawn = drawn.at[row_spot, col_spot, 0, :].set(HALO)
    drawn = drawn.at[other_row, col_spot, 0, :].set(0)
    return drawn.astype(jnp.int32)


def steps_of(rng, dims, cuts, low, largest):
    gain = 1.0
    for axis_at, parts in cuts:
        draws = jax.random.uniform(jax.random.fold_in(jax.random.fold_in(rng, 6), axis_at), (parts,), jnp.float32, low / len(cuts), largest / len(cuts))
        gain = gain * jnp.repeat(jnp.exp(draws), dims[axis_at] // parts).reshape((-1,) + (1,) * (len(dims) - 1 - axis_at))
    return gain


def bell_draw(own_key, dims, spread, reach, pieces=(), held_as=jnp.bfloat16):
    gain = steps_of(own_key, dims, pieces, -0.22, 0.18) if pieces else 1.0
    array = jax.random.normal(own_key, dims, jnp.float32) * spread * gain
    return jnp.minimum(jnp.maximum(array, -reach), reach).astype(held_as)


def setup_inputs(seed: int = 0) -> dict:
    streams_of = jax.random.split(jax.random.key(seed), 6)
    return {
        "object_field": bell_draw(streams_of[0], (2, OBJ_ROWS, OBJ_COLS), 1.0, 6.0, ((1, 16), (2, 2)), jnp.float32),
        "probe_field": bell_draw(streams_of[1], (2, WIN, WIN), 1.0, 6.0, (), jnp.float32),
        "amplitudes": jnp.clip(4.0 * jax.random.uniform(streams_of[2], (TILES_DOWN * MOST, TILES_ACROSS * WIN, WIN), jnp.float32) ** steps_of(streams_of[2], (TILES_DOWN * MOST, TILES_ACROSS * WIN, WIN), ((0, 16), (1, 2)), -0.2, 0.2), 0.0, 4.0),
        "offsets": draw_offsets(jax.random.fold_in(streams_of[5], 71), 0),
        "counts": draw_counts(jax.random.fold_in(streams_of[5], 71), 0),
    }


smooth_floor = 0.5
object_step = 0.5
tiny_value = 1e-06

def reference(object_field, probe_field, amplitudes, offsets, counts):
    blocks = amplitudes.reshape(TILES_DOWN, MOST, TILES_ACROSS, WIN, WIN)
    total_windows = TILES_DOWN * TILES_ACROSS * MOST
    current = object_field
    probe_now = probe_field
    for outer_step in range(OUTER):
        probe_cplx = probe_now[0] + 1j * probe_now[1]
        probe_mean = jnp.sum(probe_now * probe_now) / (WIN * WIN)
        probe_grad = jnp.zeros((2, WIN, WIN), jnp.float32)
        power_sum = jnp.zeros((), jnp.float32)
        for inner_step in range(INNER):
            padded = jnp.pad(current, ((0, 0), (0, HALO), (0, HALO)))

            def visit_window(running, flat_index):
                grad_grid, grad_probe, power_acc = running
                tile_row = flat_index // (TILES_ACROSS * MOST)
                tile_col = flat_index // MOST % TILES_ACROSS
                slot_index = flat_index % MOST
                first_row = (tile_row * TILE + offsets[tile_row, tile_col, slot_index, 0]).astype(jnp.int32)
                first_col = (tile_col * TILE + offsets[tile_row, tile_col, slot_index, 1]).astype(jnp.int32)
                zero_index = jnp.zeros((), jnp.int32)
                window_part = lax.dynamic_slice(padded, (zero_index, first_row, first_col), (2, WIN, WIN))
                measured = lax.dynamic_slice(blocks, (tile_row, slot_index, tile_col, zero_index, zero_index), (1, 1, 1, WIN, WIN))[0, 0, 0]
                live_flag = (slot_index < counts[tile_row, tile_col]).astype(jnp.float32)
                window_cplx = window_part[0] + 1j * window_part[1]
                spectrum = jnp.fft.fft2(probe_cplx * window_cplx, norm='ortho')
                magnitude = jnp.real(spectrum) ** 2 + jnp.imag(spectrum) ** 2
                ratio_term = measured / jnp.sqrt(magnitude + smooth_floor) - 1.0
                difference = jnp.fft.ifft2(spectrum * ratio_term, norm='ortho') * live_flag
                object_term = jnp.conj(probe_cplx) * difference
                probe_term = jnp.conj(window_cplx) * difference
                object_pair = jnp.stack([jnp.real(object_term), jnp.imag(object_term)])
                probe_pair = jnp.stack([jnp.real(probe_term), jnp.imag(probe_term)])
                present = lax.dynamic_slice(grad_grid, (zero_index, first_row, first_col), (2, WIN, WIN))
                grad_grid = lax.dynamic_update_slice(grad_grid, present + object_pair, (zero_index, first_row, first_col))
                power_acc = power_acc + live_flag * jnp.sum(window_part * window_part)
                return ((grad_grid, grad_probe + probe_pair, power_acc), None)
            start_state = (jnp.zeros_like(padded), jnp.zeros((2, WIN, WIN), jnp.float32), jnp.zeros((), jnp.float32))
            final_state, unused = lax.scan(visit_window, start_state, jnp.arange(total_windows, dtype=jnp.int32))
            grad_grid, grad_probe, power_acc = final_state
            current = current + object_step * grad_grid[:, :OBJ_ROWS, :OBJ_COLS] / (probe_mean + tiny_value)
            probe_grad = probe_grad + grad_probe
            power_sum = power_sum + power_acc
        moved_probe = probe_now + probe_grad / (power_sum / (WIN * WIN) + tiny_value)
        power_old = jnp.sum(probe_now * probe_now)
        power_new = jnp.sum(moved_probe * moved_probe)
        probe_now = moved_probe * jnp.sqrt(power_old / (power_new + tiny_value))
    return (current, probe_now)
```

```python
import functools
import math

import jax
import jax.numpy as jnp
import numpy as np
from jax import lax
from jax.experimental import pallas as pl
from jax.experimental.pallas import tpu as pltpu
from jax.sharding import PartitionSpec as P

HALO = 128
OUTER = 2


smooth_floor = 0.5
object_step = 0.5
tiny_value = 1e-06


def shifted(value, axis, by):
    length = lax.axis_size(axis)
    pairs = [(i, i + by) for i in range(length) if 0 <= i + by < length]
    return lax.ppermute(value, axis, pairs)


def make_tables(length):
    half = length // 2
    first = np.arange(half)[:, None]
    second = np.arange(half)[None, :]
    tables = []
    for parity in range(2):
        angles = (first * (2 * second + parity) % length) * (-2.0 * math.pi / length)
        real = np.cos(angles) / math.sqrt(length)
        imag = np.sin(angles) / math.sqrt(length)
        tables.append(np.block([[real, imag], [-imag, real]]))
    tables += [tables[0].T, tables[1].T]
    stacked = np.stack(tables).astype(np.float32)
    upper = stacked.astype(jnp.bfloat16)
    lower = (stacked - upper.astype(np.float32)).astype(jnp.bfloat16)
    sorting = np.zeros((length, length), np.float32)
    sorting[np.arange(length), np.arange(length) // 2 + half * (np.arange(length) % 2)] = 1.0
    return np.concatenate([upper, lower, sorting.astype(jnp.bfloat16)[None]])


def split(value):
    upper = value.astype(jnp.bfloat16)
    lower = (value - upper.astype(jnp.float32)).astype(jnp.bfloat16)
    return upper, lower


def dot(left, right):
    return jnp.dot(left, right, preferred_element_type=jnp.float32)


def times_table(value, tables, index):
    upper, lower = split(value)
    return (
        dot(upper, tables[index]) + dot(lower, tables[index]) + dot(upper, tables[index + 4])
    )


def table_times(tables, index, value):
    upper, lower = split(value)
    return (
        dot(tables[index], upper) + dot(tables[index], lower) + dot(tables[index + 4], upper)
    )


def lanes(*parts):
    return jnp.concatenate(parts, axis=1)


def stack(*parts):
    return jnp.concatenate(parts, axis=0)


def halves_of_lanes(value):
    half = value.shape[1] // 2
    return value[:, :half], value[:, half:]


def halves_of_rows(value):
    half = value.shape[0] // 2
    return value[:half], value[half:]


def forward(real, imag, tables):
    real_l, real_r = halves_of_lanes(real)
    imag_l, imag_r = halves_of_lanes(imag)
    even = times_table(lanes(real_l + real_r, imag_l + imag_r), tables, 0)
    odd = times_table(lanes(real_l - real_r, imag_l - imag_r), tables, 1)
    even_t, even_b = halves_of_rows(even)
    odd_t, odd_b = halves_of_rows(odd)
    even_re, even_im = halves_of_lanes(even_t + even_b)
    odd_re, odd_im = halves_of_lanes(odd_t + odd_b)
    top = table_times(tables, 2, stack(lanes(even_re, odd_re), lanes(even_im, odd_im)))
    even_re, even_im = halves_of_lanes(even_t - even_b)
    odd_re, odd_im = halves_of_lanes(odd_t - odd_b)
    bottom = table_times(tables, 3, stack(lanes(even_re, odd_re), lanes(even_im, odd_im)))
    return top, bottom


def inverse(top, bottom, tables):
    top = table_times(tables, 0, top)
    bottom = table_times(tables, 1, bottom)
    upper_re, upper_im = halves_of_rows(top + bottom)
    lower_re, lower_im = halves_of_rows(top - bottom)
    even_ur, odd_ur = halves_of_lanes(upper_re)
    even_ui, odd_ui = halves_of_lanes(upper_im)
    even_lr, odd_lr = halves_of_lanes(lower_re)
    even_li, odd_li = halves_of_lanes(lower_im)
    even = times_table(stack(lanes(even_ur, even_ui), lanes(even_lr, even_li)), tables, 2)
    odd = times_table(stack(lanes(odd_ur, odd_ui), lanes(odd_lr, odd_li)), tables, 3)
    left_re, left_im = halves_of_lanes(even + odd)
    right_re, right_im = halves_of_lanes(even - odd)
    return lanes(left_re, right_re), lanes(left_im, right_im)


def sorted_amplitudes(amp_ref, slot, tables, hold):
    upper, lower = split(amp_ref[slot])
    value = dot(upper, tables[8]) + dot(lower, tables[8])
    left, right = halves_of_lanes(value)
    hold[0] = left
    hold[1] = right
    half = value.shape[0] // 2
    return [
        lanes(
            hold[0, pl.ds(parity, half, stride=2), :], hold[1, pl.ds(parity, half, stride=2), :]
        )
        for parity in range(2)
    ]


def cut_window(slabs, part, first_row, first_col, window, margin):
    lane = lax.broadcasted_iota(jnp.int32, (window, margin), 1)
    inside = lane < margin - first_col
    turn = lax.rem(margin - first_col, margin)
    turned = [
        pltpu.roll(slabs[part, slab, pl.ds(first_row, window), :], turn, 1)
        for slab in range(slabs.shape[1])
    ]
    return lanes(*[jnp.where(inside, a, b) for a, b in zip(turned[:-1], turned[1:])])


def place_lanes(term, first_col, margin):
    window = term.shape[0]
    lane = lax.broadcasted_iota(jnp.int32, (window, margin), 1)
    inside = lane >= first_col
    turn = lax.rem(first_col, margin)
    turned = [
        pltpu.roll(term[:, at : at + margin], turn, 1) for at in range(0, term.shape[1], margin)
    ]
    empty = jnp.zeros((window, margin), term.dtype)
    return [jnp.where(inside, a, b) for a, b in zip(turned + [empty], [empty] + turned)]


def pass_over_windows(
    off_ref, cnt_ref, ext_ref, probe_ref, amp_ref, tables, grad_ref, pgrad_ref, hold, slabs, padded
):
    slot_count = amp_ref.shape[0]
    window = probe_ref.shape[1]
    ext_rows = ext_ref.shape[1]
    margin = ext_rows - window
    for part in range(2):
        for slab in range(slabs.shape[1]):
            slabs[part, slab] = ext_ref[part, :, slab * margin : (slab + 1) * margin]
    probe_re = probe_ref[0]
    probe_im = probe_ref[1]
    power = None
    for slot in range(slot_count):
        first_row = off_ref[0, 0, slot, 0]
        first_col = off_ref[0, 0, slot, 1]
        live = (slot < cnt_ref[0, 0]).astype(jnp.float32)
        win_re = cut_window(slabs, 0, first_row, first_col, window, margin)
        win_im = cut_window(slabs, 1, first_row, first_col, window, margin)
        spectrum = forward(
            probe_re * win_re - probe_im * win_im, probe_re * win_im + probe_im * win_re, tables
        )
        replaced = []
        for hat, measured in zip(spectrum, sorted_amplitudes(amp_ref, slot, tables, hold.at[slot])):
            hat_re, hat_im = halves_of_rows(hat)
            ratio = measured * lax.rsqrt(hat_re * hat_re + hat_im * hat_im + smooth_floor) - 1.0
            ratio = ratio * live
            replaced.append(stack(hat_re * ratio, hat_im * ratio))
        diff_re, diff_im = inverse(*replaced, tables)
        terms = (probe_re * diff_re + probe_im * diff_im, probe_re * diff_im - probe_im * diff_re)
        for part, term in enumerate(terms):
            empty = jnp.zeros((margin, margin), jnp.float32)
            for slab, placed in enumerate(place_lanes(term, first_col, margin)):
                box = padded.at[slot, part, slab]
                box[:margin] = empty
                box[margin : margin + window] = placed
                box[margin + window :] = empty
                shown = box[pl.ds(margin - first_row, ext_rows), :]
                here = slice(slab * margin, (slab + 1) * margin)
                if slot == 0:
                    grad_ref[part, :, here] = shown
                else:
                    grad_ref[part, :, here] += shown
        probe_terms = (win_re * diff_re + win_im * diff_im, win_re * diff_im - win_im * diff_re)
        for part, term in enumerate(probe_terms):
            pgrad_ref[part] = term if slot == 0 else pgrad_ref[part] + term
        squares = jnp.sum(win_re * win_re + win_im * win_im, axis=0, keepdims=True) * live
        power = squares if power is None else power + squares
    return power


def pass_kernel(
    off_ref, cnt_ref, ext_ref, probe_ref, amp_ref, tables, grad_ref, pgrad_ref, power_ref, *scratch
):
    power = pass_over_windows(
        off_ref, cnt_ref, ext_ref, probe_ref, amp_ref, tables, grad_ref, pgrad_ref, *scratch
    )
    power_ref[...] = jnp.broadcast_to(power, power_ref.shape)


def one_pass(extended, probe, amplitudes, offsets, counts, tables):
    slots, window = amplitudes.shape[0], probe.shape[1]
    ext_rows, ext_cols = extended.shape[1:]
    margin = ext_rows - window
    smem = pl.BlockSpec(memory_space=pltpu.SMEM)
    vmem = pl.BlockSpec(memory_space=pltpu.VMEM)
    return pl.pallas_call(
        pass_kernel,
        out_shape=(
            jax.ShapeDtypeStruct(extended.shape, jnp.float32),
            jax.ShapeDtypeStruct(probe.shape, jnp.float32),
            jax.ShapeDtypeStruct((8, window), jnp.float32),
        ),
        in_specs=[smem, smem, vmem, vmem, vmem, vmem],
        out_specs=(vmem, vmem, vmem),
        scratch_shapes=[
            pltpu.VMEM((slots, 2, window, window // 2), jnp.float32),
            pltpu.VMEM((2, ext_cols // margin, ext_rows, margin), jnp.float32),
            pltpu.VMEM((slots, 2, ext_cols // margin, window + 2 * margin, margin), jnp.float32),
        ],
        compiler_params=pltpu.CompilerParams(vmem_limit_bytes=40 * 2**20),
        name="window_pass",
    )(offsets, counts, extended, probe, amplitudes, tables)


def shards(object_field, probe_field, amplitudes, offsets, counts):
    tile_rows = object_field.shape[1]
    tile_cols = object_field.shape[2]
    window = probe_field.shape[1]
    margin = HALO
    tables = jnp.asarray(make_tables(window))
    current = object_field
    probe_now = probe_field
    for outer_step in range(OUTER):
        probe_mean = jnp.sum(probe_now * probe_now) / (window * window)
        lower_rows = shifted(current[:, :margin, :], "row", -1)
        taller = jnp.concatenate([current, lower_rows], axis=1)
        right_cols = shifted(taller[:, :, :margin], "col", -1)
        extended = jnp.concatenate([taller, right_cols], axis=2)
        grad_ext, probe_grad, power = one_pass(
            extended, probe_now, amplitudes, offsets, counts, tables
        )
        rim_right = shifted(grad_ext[:, :, tile_cols:], "col", 1)
        narrowed = grad_ext[:, :, :tile_cols]
        narrowed = jnp.concatenate(
            [narrowed[:, :, :margin] + rim_right, narrowed[:, :, margin:]], axis=2
        )
        rim_lower = shifted(narrowed[:, tile_rows:, :], "row", 1)
        tile_grad = jnp.concatenate(
            [narrowed[:, :margin, :] + rim_lower, narrowed[:, margin:tile_rows, :]], axis=1
        )
        current = current + object_step * tile_grad / (probe_mean + tiny_value)
        power_old = jnp.sum(probe_now * probe_now)
        summed_grad, summed_power = lax.psum((probe_grad, power[0]), ("row", "col"))
        moved_probe = probe_now + summed_grad / (
            jnp.sum(summed_power) / (window * window) + tiny_value
        )
        power_new = jnp.sum(moved_probe * moved_probe)
        probe_now = moved_probe * jnp.sqrt(power_old / (power_new + tiny_value))
    return (current, probe_now)


def solution(mesh):
    return jax.shard_map(
        shards,
        mesh=mesh,
        in_specs=(
            P(None, "row", "col"),
            P(),
            P("row", "col", None),
            P("row", "col", None, None),
            P("row", "col"),
        ),
        out_specs=(P(None, "row", "col"), P()),
        check_vma=False,
    )
```

```python
import functools
import math

import jax
import jax.numpy as jnp
import numpy as np
from jax import lax
from jax.experimental import pallas as pl
from jax.experimental.pallas import tpu as pltpu
from jax.sharding import PartitionSpec as P

MESH = pl.DeviceIdType.MESH
HALO = 128
OUTER = 2


smooth_floor = 0.5
object_step = 0.5
tiny_value = 1e-06


def shifted(value, axis, by):
    length = lax.axis_size(axis)
    pairs = [(i, i + by) for i in range(length) if 0 <= i + by < length]
    return lax.ppermute(value, axis, pairs)


def make_tables(length):
    half = length // 2
    first = np.arange(half)[:, None]
    second = np.arange(half)[None, :]
    tables = []
    for parity in range(2):
        angles = (first * (2 * second + parity) % length) * (-2.0 * math.pi / length)
        real = np.cos(angles) / math.sqrt(length)
        imag = np.sin(angles) / math.sqrt(length)
        tables.append(np.block([[real, imag], [-imag, real]]))
    tables += [tables[0].T, tables[1].T]
    stacked = np.stack(tables).astype(np.float32)
    upper = stacked.astype(jnp.bfloat16)
    lower = (stacked - upper.astype(np.float32)).astype(jnp.bfloat16)
    sorting = np.zeros((length, length), np.float32)
    sorting[np.arange(length), np.arange(length) // 2 + half * (np.arange(length) % 2)] = 1.0
    return np.concatenate([upper, lower, sorting.astype(jnp.bfloat16)[None]])


def split(value):
    upper = value.astype(jnp.bfloat16)
    lower = (value - upper.astype(jnp.float32)).astype(jnp.bfloat16)
    return upper, lower


def dot(left, right):
    return jnp.dot(left, right, preferred_element_type=jnp.float32)


def times_table(value, tables, index):
    upper, lower = split(value)
    return (
        dot(upper, tables[index]) + dot(lower, tables[index]) + dot(upper, tables[index + 4])
    )


def table_times(tables, index, value):
    upper, lower = split(value)
    return (
        dot(tables[index], upper) + dot(tables[index], lower) + dot(tables[index + 4], upper)
    )


def lanes(*parts):
    return jnp.concatenate(parts, axis=1)


def stack(*parts):
    return jnp.concatenate(parts, axis=0)


def halves_of_lanes(value):
    half = value.shape[1] // 2
    return value[:, :half], value[:, half:]


def halves_of_rows(value):
    half = value.shape[0] // 2
    return value[:half], value[half:]


def forward(real, imag, tables):
    real_l, real_r = halves_of_lanes(real)
    imag_l, imag_r = halves_of_lanes(imag)
    even = times_table(lanes(real_l + real_r, imag_l + imag_r), tables, 0)
    odd = times_table(lanes(real_l - real_r, imag_l - imag_r), tables, 1)
    even_t, even_b = halves_of_rows(even)
    odd_t, odd_b = halves_of_rows(odd)
    even_re, even_im = halves_of_lanes(even_t + even_b)
    odd_re, odd_im = halves_of_lanes(odd_t + odd_b)
    top = table_times(tables, 2, stack(lanes(even_re, odd_re), lanes(even_im, odd_im)))
    even_re, even_im = halves_of_lanes(even_t - even_b)
    odd_re, odd_im = halves_of_lanes(odd_t - odd_b)
    bottom = table_times(tables, 3, stack(lanes(even_re, odd_re), lanes(even_im, odd_im)))
    return top, bottom


def inverse(top, bottom, tables):
    top = table_times(tables, 0, top)
    bottom = table_times(tables, 1, bottom)
    upper_re, upper_im = halves_of_rows(top + bottom)
    lower_re, lower_im = halves_of_rows(top - bottom)
    even_ur, odd_ur = halves_of_lanes(upper_re)
    even_ui, odd_ui = halves_of_lanes(upper_im)
    even_lr, odd_lr = halves_of_lanes(lower_re)
    even_li, odd_li = halves_of_lanes(lower_im)
    even = times_table(stack(lanes(even_ur, even_ui), lanes(even_lr, even_li)), tables, 2)
    odd = times_table(stack(lanes(odd_ur, odd_ui), lanes(odd_lr, odd_li)), tables, 3)
    left_re, left_im = halves_of_lanes(even + odd)
    right_re, right_im = halves_of_lanes(even - odd)
    return lanes(left_re, right_re), lanes(left_im, right_im)


def sorted_amplitudes(amp_ref, slot, tables, hold):
    upper, lower = split(amp_ref[slot])
    value = dot(upper, tables[8]) + dot(lower, tables[8])
    left, right = halves_of_lanes(value)
    hold[0] = left
    hold[1] = right
    half = value.shape[0] // 2
    return [
        lanes(
            hold[0, pl.ds(parity, half, stride=2), :], hold[1, pl.ds(parity, half, stride=2), :]
        )
        for parity in range(2)
    ]


def cut_window(slabs, part, first_row, first_col, window, margin):
    lane = lax.broadcasted_iota(jnp.int32, (window, margin), 1)
    inside = lane < margin - first_col
    turn = lax.rem(margin - first_col, margin)
    turned = [
        pltpu.roll(slabs[part, slab, pl.ds(first_row, window), :], turn, 1)
        for slab in range(slabs.shape[1])
    ]
    return lanes(*[jnp.where(inside, a, b) for a, b in zip(turned[:-1], turned[1:])])


def place_lanes(term, first_col, margin):
    window = term.shape[0]
    lane = lax.broadcasted_iota(jnp.int32, (window, margin), 1)
    inside = lane >= first_col
    turn = lax.rem(first_col, margin)
    turned = [
        pltpu.roll(term[:, at : at + margin], turn, 1) for at in range(0, term.shape[1], margin)
    ]
    empty = jnp.zeros((window, margin), term.dtype)
    return [jnp.where(inside, a, b) for a, b in zip(turned + [empty], [empty] + turned)]


def pass_over_windows(
    off_ref, cnt_ref, ext_ref, probe_ref, amp_ref, tables, grad_ref, pgrad_ref, hold, slabs, padded
):
    slot_count = amp_ref.shape[0]
    window = probe_ref.shape[1]
    ext_rows = ext_ref.shape[1]
    margin = ext_rows - window
    for part in range(2):
        for slab in range(slabs.shape[1]):
            slabs[part, slab] = ext_ref[part, :, slab * margin : (slab + 1) * margin]
    probe_re = probe_ref[0]
    probe_im = probe_ref[1]
    power = None
    for slot in range(slot_count):
        first_row = off_ref[0, 0, slot, 0]
        first_col = off_ref[0, 0, slot, 1]
        live = (slot < cnt_ref[0, 0]).astype(jnp.float32)
        win_re = cut_window(slabs, 0, first_row, first_col, window, margin)
        win_im = cut_window(slabs, 1, first_row, first_col, window, margin)
        spectrum = forward(
            probe_re * win_re - probe_im * win_im, probe_re * win_im + probe_im * win_re, tables
        )
        replaced = []
        for hat, measured in zip(spectrum, sorted_amplitudes(amp_ref, slot, tables, hold.at[slot])):
            hat_re, hat_im = halves_of_rows(hat)
            ratio = measured * lax.rsqrt(hat_re * hat_re + hat_im * hat_im + smooth_floor) - 1.0
            ratio = ratio * live
            replaced.append(stack(hat_re * ratio, hat_im * ratio))
        diff_re, diff_im = inverse(*replaced, tables)
        terms = (probe_re * diff_re + probe_im * diff_im, probe_re * diff_im - probe_im * diff_re)
        for part, term in enumerate(terms):
            empty = jnp.zeros((margin, margin), jnp.float32)
            for slab, placed in enumerate(place_lanes(term, first_col, margin)):
                box = padded.at[slot, part, slab]
                box[:margin] = empty
                box[margin : margin + window] = placed
                box[margin + window :] = empty
                shown = box[pl.ds(margin - first_row, ext_rows), :]
                here = slice(slab * margin, (slab + 1) * margin)
                if slot == 0:
                    grad_ref[part, :, here] = shown
                else:
                    grad_ref[part, :, here] += shown
        probe_terms = (win_re * diff_re + win_im * diff_im, win_re * diff_im - win_im * diff_re)
        for part, term in enumerate(probe_terms):
            pgrad_ref[part] = term if slot == 0 else pgrad_ref[part] + term
        squares = jnp.sum(win_re * win_re + win_im * win_im, axis=0, keepdims=True) * live
        power = squares if power is None else power + squares
    return power


def pass_kernel(
    off_ref, cnt_ref, ext_ref, probe_ref, amp_ref, tables, grad_ref, pgrad_ref, power_ref, *scratch
):
    power = pass_over_windows(
        off_ref, cnt_ref, ext_ref, probe_ref, amp_ref, tables, grad_ref, pgrad_ref, *scratch
    )
    power_ref[...] = jnp.broadcast_to(power, power_ref.shape)


def one_pass(extended, probe, amplitudes, offsets, counts, tables):
    slots, window = amplitudes.shape[0], probe.shape[1]
    ext_rows, ext_cols = extended.shape[1:]
    margin = ext_rows - window
    smem = pl.BlockSpec(memory_space=pltpu.SMEM)
    vmem = pl.BlockSpec(memory_space=pltpu.VMEM)
    return pl.pallas_call(
        pass_kernel,
        out_shape=(
            jax.ShapeDtypeStruct(extended.shape, jnp.float32),
            jax.ShapeDtypeStruct(probe.shape, jnp.float32),
            jax.ShapeDtypeStruct((8, window), jnp.float32),
        ),
        in_specs=[smem, smem, vmem, vmem, vmem, vmem],
        out_specs=(vmem, vmem, vmem),
        scratch_shapes=[
            pltpu.VMEM((slots, 2, window, window // 2), jnp.float32),
            pltpu.VMEM((2, ext_cols // margin, ext_rows, margin), jnp.float32),
            pltpu.VMEM((slots, 2, ext_cols // margin, window + 2 * margin, margin), jnp.float32),
        ],
        compiler_params=pltpu.CompilerParams(vmem_limit_bytes=40 * 2**20),
        name="window_pass",
    )(offsets, counts, extended, probe, amplitudes, tables)


def remote(src, dst, send_sem, recv_sem, **where):
    return pltpu.make_async_remote_copy(
        src_ref=src,
        dst_ref=dst,
        send_sem=send_sem,
        recv_sem=recv_sem,
        device_id=where,
        device_id_type=MESH,
    )


class Place:
    def __init__(self):
        self.rows = lax.axis_size("row")
        self.cols = lax.axis_size("col")
        self.row = lax.axis_index("row")
        self.col = lax.axis_index("col")
        self.has_up = self.row > 0
        self.has_down = self.row < self.rows - 1
        self.has_left = self.col > 0
        self.has_right = self.col < self.cols - 1
        self.up = lax.max(self.row - 1, 0)
        self.down = lax.min(self.row + 1, self.rows - 1)
        self.left = lax.max(self.col - 1, 0)
        self.right = lax.min(self.col + 1, self.cols - 1)

    def other_row(self, step):
        return lax.rem(self.row + step, self.rows)

    def other_col(self, step):
        return lax.rem(self.col + step, self.cols)

    def greet(self):
        barrier = pltpu.get_barrier_semaphore()
        for step in range(1, self.cols):
            pl.semaphore_signal(
                barrier, inc=1, device_id={"col": self.other_col(step)}, device_id_type=MESH
            )
        for step in range(1, self.rows):
            pl.semaphore_signal(
                barrier, inc=1, device_id={"row": self.other_row(step)}, device_id_type=MESH
            )

    def await_greetings(self):
        pl.semaphore_wait(pltpu.get_barrier_semaphore(), self.rows + self.cols - 2)


class Halo:
    @staticmethod
    def scratch(tile_rows, tile_cols, margin):
        return [
            pltpu.VMEM((2, margin, tile_cols), jnp.float32),
            pltpu.VMEM((2, tile_rows, margin), jnp.float32),
            pltpu.VMEM((2, margin, margin), jnp.float32),
            pltpu.SemaphoreType.DMA((3,)),
            pltpu.SemaphoreType.DMA((3,)),
        ]

    def __init__(self, place, object_ref, below, beside, corner, sent, came):
        self.place, self.object_ref = place, object_ref
        self.below, self.beside, self.corner = below, beside, corner
        margin = corner.shape[1]
        self.margin = margin
        self.from_below = remote(
            object_ref.at[:, pl.ds(0, margin), :], below, sent.at[0], came.at[0], row=place.up
        )
        self.from_beside = remote(
            object_ref.at[:, :, pl.ds(0, margin)], beside, sent.at[1], came.at[1], col=place.left
        )
        self.from_corner = remote(
            below.at[:, :, pl.ds(0, margin)], corner, sent.at[2], came.at[2], col=place.left
        )

    def start(self):
        pl.when(self.place.has_up)(self.from_below.start)
        pl.when(self.place.has_left)(self.from_beside.start)

    def finish(self, ext_ref):
        place, margin = self.place, self.margin
        _, tile_rows, tile_cols = self.object_ref.shape
        ext_ref[:, :tile_rows, :tile_cols] = self.object_ref[...]

        @pl.when(place.has_down)
        def _():
            self.from_below.wait_recv()
            pl.when(place.has_left)(self.from_corner.start)
            ext_ref[:, tile_rows:, :tile_cols] = self.below[...]

        @pl.when(jnp.logical_not(place.has_down))
        def _():
            ext_ref[:, tile_rows:, :] = jnp.zeros((2, margin, tile_cols + margin), jnp.float32)

        @pl.when(place.has_right)
        def _():
            self.from_beside.wait_recv()
            ext_ref[:, :tile_rows, tile_cols:] = self.beside[...]

            @pl.when(place.has_down)
            def _():
                self.from_corner.wait_recv()
                ext_ref[:, tile_rows:, tile_cols:] = self.corner[...]

        @pl.when(jnp.logical_not(place.has_right))
        def _():
            ext_ref[:, :, tile_cols:] = jnp.zeros((2, tile_rows + margin, margin), jnp.float32)

    def settle(self):
        place = self.place
        pl.when(place.has_up)(self.from_below.wait_send)
        pl.when(place.has_left)(self.from_beside.wait_send)
        pl.when(jnp.logical_and(place.has_left, place.has_down))(self.from_corner.wait_send)


class Rims:
    @staticmethod
    def scratch(tile_rows, tile_cols, margin):
        tall, wide = tile_rows + margin, tile_cols + margin
        return [
            pltpu.VMEM((2, tall, wide), jnp.float32),
            pltpu.VMEM((2, tall, margin), jnp.float32),
            pltpu.VMEM((2, tall, margin), jnp.float32),
            pltpu.VMEM((2, margin, tile_cols), jnp.float32),
            pltpu.VMEM((2, margin, tile_cols), jnp.float32),
            pltpu.VMEM((2, margin, margin), jnp.float32),
            pltpu.VMEM((2, margin, margin), jnp.float32),
            pltpu.SemaphoreType.DMA((6,)),
            pltpu.SemaphoreType.DMA((6,)),
        ]

    def __init__(self, place, last, grad, total, left, right, above, below, over, under, sent, came):
        self.place, self.last, self.grad, self.total = place, last, grad, total
        self.left, self.right, self.above, self.below = left, right, above, below
        self.over, self.under = over, under
        margin = over.shape[1]
        tile_rows, tile_cols = grad.shape[1] - margin, grad.shape[2] - margin
        self.sizes = margin, tile_rows, tile_cols
        first, own = pl.ds(0, margin), pl.ds(0, tile_cols)
        self.to_right = remote(
            grad.at[:, :, pl.ds(tile_cols, margin)], left, sent.at[0], came.at[0], col=place.right
        )
        self.to_left = remote(grad.at[:, :, first], right, sent.at[1], came.at[1], col=place.left)
        self.to_down = remote(
            total.at[:, pl.ds(tile_rows, margin), own], above, sent.at[2], came.at[2], row=place.down
        )
        self.to_up = remote(total.at[:, first, own], below, sent.at[3], came.at[3], row=place.up)
        self.pass_over = remote(
            above.at[:, :, first], over, sent.at[4], came.at[4], col=place.left
        )
        self.pass_under = remote(
            below.at[:, :, first], under, sent.at[5], came.at[5], col=place.left
        )

    def start(self):
        pl.when(self.place.has_right)(self.to_right.start)
        if not self.last:
            pl.when(self.place.has_left)(self.to_left.start)

    def start_rows(self):
        place, grad, total = self.place, self.grad, self.total
        margin, tile_rows, tile_cols = self.sizes
        total[...] = grad[...]

        @pl.when(place.has_left)
        def _():
            self.to_right.wait_recv()
            total[:, :, :margin] += self.left[...]

        if not self.last:

            @pl.when(place.has_right)
            def _():
                self.to_left.wait_recv()
                total[:, :, tile_cols:] += self.right[...]

        pl.when(place.has_down)(self.to_down.start)
        if not self.last:
            pl.when(place.has_up)(self.to_up.start)

    def finish(self, old_ref, new_ref, factor):
        place, total = self.place, self.total
        margin, tile_rows, tile_cols = self.sizes
        new_ref[:, margin:tile_rows, :tile_cols] = (
            old_ref[:, margin:tile_rows, :tile_cols] + factor * total[:, margin:tile_rows, :tile_cols]
        )

        @pl.when(place.has_up)
        def _():
            self.to_down.wait_recv()
            if not self.last:
                pl.when(place.has_left)(self.pass_over.start)
            new_ref[:, :margin, :tile_cols] = old_ref[:, :margin, :tile_cols] + factor * (
                total[:, :margin, :tile_cols] + self.above[...]
            )

        @pl.when(jnp.logical_not(place.has_up))
        def _():
            new_ref[:, :margin, :tile_cols] = (
                old_ref[:, :margin, :tile_cols] + factor * total[:, :margin, :tile_cols]
            )

        if self.last:
            return

        @pl.when(place.has_down)
        def _():
            self.to_up.wait_recv()
            pl.when(place.has_left)(self.pass_under.start)
            new_ref[:, tile_rows:, :tile_cols] = old_ref[:, tile_rows:, :tile_cols] + factor * (
                total[:, tile_rows:, :tile_cols] + self.below[...]
            )

        @pl.when(jnp.logical_not(place.has_down))
        def _():
            new_ref[:, tile_rows:, :] = jnp.zeros((2, margin, tile_cols + margin), jnp.float32)

        @pl.when(place.has_right)
        def _():
            new_ref[:, margin:tile_rows, tile_cols:] = (
                old_ref[:, margin:tile_rows, tile_cols:]
                + factor * total[:, margin:tile_rows, tile_cols:]
            )

            @pl.when(place.has_up)
            def _():
                self.pass_over.wait_recv()
                new_ref[:, :margin, tile_cols:] = old_ref[:, :margin, tile_cols:] + factor * (
                    total[:, :margin, tile_cols:] + self.over[...]
                )

            @pl.when(jnp.logical_not(place.has_up))
            def _():
                new_ref[:, :margin, tile_cols:] = (
                    old_ref[:, :margin, tile_cols:] + factor * total[:, :margin, tile_cols:]
                )

            @pl.when(place.has_down)
            def _():
                self.pass_under.wait_recv()
                new_ref[:, tile_rows:, tile_cols:] = old_ref[:, tile_rows:, tile_cols:] + factor * (
                    total[:, tile_rows:, tile_cols:] + self.under[...]
                )

        @pl.when(jnp.logical_not(place.has_right))
        def _():
            new_ref[:, :, tile_cols:] = jnp.zeros((2, tile_rows + margin, margin), jnp.float32)

    def settle(self):
        place = self.place
        pl.when(place.has_right)(self.to_right.wait_send)
        pl.when(place.has_down)(self.to_down.wait_send)
        if not self.last:
            pl.when(place.has_left)(self.to_left.wait_send)
            pl.when(place.has_up)(self.to_up.wait_send)
            pl.when(jnp.logical_and(place.has_left, place.has_up))(self.pass_over.wait_send)
            pl.when(jnp.logical_and(place.has_left, place.has_down))(self.pass_under.wait_send)


class Sums:
    extra = 8

    @staticmethod
    def chunk(rows, cols, window):
        return 2 * window * window // 128 // (rows * cols)

    @classmethod
    def scratch(cls, rows, cols, window):
        deep = cls.chunk(rows, cols, window)
        full = deep + cls.extra
        more_cols, more_rows = max(cols - 1, 1), rows - 1
        return [
            pltpu.VMEM((cols, rows, full, 128), jnp.float32),
            pltpu.VMEM((more_cols, rows, full, 128), jnp.float32),
            pltpu.VMEM((rows, full, 128), jnp.float32),
            pltpu.VMEM((more_rows, full, 128), jnp.float32),
            pltpu.VMEM((cols, rows, deep, 128), jnp.float32),
            pltpu.SemaphoreType.DMA((2, more_cols)),
            pltpu.SemaphoreType.DMA((2, more_rows)),
            pltpu.SemaphoreType.DMA((2, more_rows)),
            pltpu.SemaphoreType.DMA((2, more_cols, rows)),
        ]

    def __init__(self, place, whole, from_cols, part, from_rows, gathered, sems, sems2, sems3, sems4):
        self.place, self.whole, self.from_cols, self.part = place, whole, from_cols, part
        self.from_rows, self.gathered = from_rows, gathered
        self.deep = gathered.shape[2]
        self.over_cols = [
            remote(
                whole.at[place.other_col(step)],
                from_cols.at[step - 1],
                sems.at[0, step - 1],
                sems.at[1, step - 1],
                col=place.other_col(step),
            )
            for step in range(1, place.cols)
        ]
        self.over_rows = [
            remote(
                part.at[place.other_row(step)],
                from_rows.at[step - 1],
                sems2.at[0, step - 1],
                sems2.at[1, step - 1],
                row=place.other_row(step),
            )
            for step in range(1, place.rows)
        ]
        mine = gathered.at[place.col, place.row]
        self.back_rows = [
            remote(
                mine,
                mine,
                sems3.at[0, step - 1],
                sems3.at[1, step - 1],
                row=place.other_row(step),
            )
            for step in range(1, place.rows)
        ]
        self.back_cols = []
        for step in range(place.rows):
            chunk = gathered.at[place.col, place.other_row(place.rows - step)]
            self.back_cols.append(
                [
                    remote(
                        chunk,
                        chunk,
                        sems4.at[0, other - 1, step],
                        sems4.at[1, other - 1, step],
                        col=place.other_col(other),
                    )
                    for other in range(1, place.cols)
                ]
            )

    def slots(self, window):
        per = window // self.deep
        for number in range(self.place.cols * self.place.rows):
            slab, at = divmod(number, per)
            half, col = divmod(slab, window // 128)
            yield half, col * 128, at * self.deep, number // self.place.rows, number % self.place.rows

    def fill(self, pgrad_ref, power):
        window = pgrad_ref.shape[1]
        for half, lane, line, col, row in self.slots(window):
            self.whole[col, row, : self.deep] = pgrad_ref[
                half, line : line + self.deep, lane : lane + 128
            ]
        folded = sum(power[:, at : at + 128] for at in range(0, window, 128))
        first = lax.broadcasted_iota(jnp.int32, (self.extra, 128), 0) == 0
        block = jnp.where(first, jnp.broadcast_to(folded, (self.extra, 128)), 0.0)
        for col in range(self.place.cols):
            for row in range(self.place.rows):
                self.whole[col, row, self.deep :] = block

    def start(self):
        for copy in self.over_cols:
            copy.start()

    def start_rows(self):
        self.part[...] = self.whole[self.place.col]
        for step, copy in enumerate(self.over_cols):
            copy.wait_recv()
            self.part[...] += self.from_cols[step]
        for copy in self.over_rows:
            copy.start()

    def start_back(self):
        total = self.part[self.place.row]
        for step, copy in enumerate(self.over_rows):
            copy.wait_recv()
            total = total + self.from_rows[step]
        self.gathered[self.place.col, self.place.row] = total[: self.deep]
        for copy in self.back_rows + self.back_cols[0]:
            copy.start()
        return jnp.sum(total[self.deep :])

    def pass_on(self):
        for step, copy in enumerate(self.back_rows):
            copy.wait_recv()
            for other in self.back_cols[step + 1]:
                other.start()

    def finish(self, power, probe_ref, new_ref):
        window = probe_ref.shape[1]
        for copies in self.back_cols:
            for copy in copies:
                copy.wait_recv()
        old = jnp.sum(probe_ref[...] * probe_ref[...], keepdims=True)
        scale = 1.0 / (power / (window * window) + tiny_value)
        for half, lane, line, col, row in self.slots(window):
            here = (half, slice(line, line + self.deep), slice(lane, lane + 128))
            moved = probe_ref[here] + self.gathered[col, row] * scale
            new_ref[here] = moved
        moved = new_ref[...]
        new = jnp.sum(moved * moved, keepdims=True)
        new_ref[...] = moved * jnp.sqrt(old / (new + tiny_value))

    def settle(self):
        for copy in self.over_cols + self.over_rows + self.back_rows:
            copy.wait_send()
        for copies in self.back_cols:
            for copy in copies:
                copy.wait_send()


def halo_kernel(object_ref, ext_ref, *scratch):
    place = Place()
    place.greet()
    halo = Halo(place, object_ref, *scratch)
    place.await_greetings()
    halo.start()
    halo.finish(ext_ref)
    halo.settle()


def exchange_kernel(
    rim_scratch, last, grad_ref, pgrad_ref, power_ref, ext_ref, probe_ref, out_ref, new_ref, *scratch
):
    place = Place()
    place.greet()
    rims = Rims(place, last, grad_ref, *scratch[:rim_scratch])
    sums = Sums(place, *scratch[rim_scratch:])
    sums.fill(pgrad_ref, power_ref[0:1])
    place.await_greetings()
    exchange(rims, sums, ext_ref, probe_ref, out_ref, new_ref)


def exchange(rims, sums, ext_ref, probe_ref, out_ref, new_ref):
    window = probe_ref.shape[1]
    sums.start()
    rims.start()
    sums.start_rows()
    rims.start_rows()
    power = sums.start_back()
    mean = jnp.sum(probe_ref[...] * probe_ref[...]) / (window * window)
    rims.finish(ext_ref, out_ref, object_step / (mean + tiny_value))
    sums.pass_on()
    sums.finish(power, probe_ref, new_ref)
    rims.settle()
    sums.settle()


def kernel_params(number):
    return pltpu.CompilerParams(
        collective_id=number, has_side_effects=True, vmem_limit_bytes=40 * 2**20
    )


def begin(object_field, margin):
    _, tile_rows, tile_cols = object_field.shape
    vmem = pl.BlockSpec(memory_space=pltpu.VMEM)
    return pl.pallas_call(
        halo_kernel,
        out_shape=jax.ShapeDtypeStruct((2, tile_rows + margin, tile_cols + margin), jnp.float32),
        in_specs=[vmem],
        out_specs=vmem,
        scratch_shapes=Halo.scratch(tile_rows, tile_cols, margin),
        compiler_params=kernel_params(0),
        name="first_halo",
    )(object_field)


def exchanged(last, margin, grad_ext, probe_grad, power, extended, probe):
    tile_rows, tile_cols = extended.shape[1] - margin, extended.shape[2] - margin
    rows, cols, window = lax.axis_size("row"), lax.axis_size("col"), probe.shape[1]
    vmem = pl.BlockSpec(memory_space=pltpu.VMEM)
    rim_scratch = Rims.scratch(tile_rows, tile_cols, margin)
    out = (2, tile_rows, tile_cols) if last else extended.shape
    return pl.pallas_call(
        functools.partial(exchange_kernel, len(rim_scratch), last),
        out_shape=(
            jax.ShapeDtypeStruct(out, jnp.float32),
            jax.ShapeDtypeStruct(probe.shape, jnp.float32),
        ),
        in_specs=[vmem] * 5,
        out_specs=(vmem, vmem),
        scratch_shapes=rim_scratch + Sums.scratch(rows, cols, window),
        compiler_params=kernel_params(2 if last else 1),
        name="last_exchange" if last else "exchange",
    )(grad_ext, probe_grad, power, extended, probe)


def shards_by_kernels(object_field, probe_field, amplitudes, offsets, counts):
    tables = jnp.asarray(make_tables(probe_field.shape[1]))
    extended = begin(object_field, HALO)
    probe = probe_field
    for outer_step in range(OUTER):
        terms = one_pass(extended, probe, amplitudes, offsets, counts, tables)
        extended, probe = exchanged(outer_step == OUTER - 1, HALO, *terms, extended, probe)
    return (extended, probe)


def shards(object_field, probe_field, amplitudes, offsets, counts):
    tile_rows = object_field.shape[1]
    tile_cols = object_field.shape[2]
    window = probe_field.shape[1]
    margin = HALO
    tables = jnp.asarray(make_tables(window))
    current = object_field
    probe_now = probe_field
    for outer_step in range(OUTER):
        probe_mean = jnp.sum(probe_now * probe_now) / (window * window)
        lower_rows = shifted(current[:, :margin, :], "row", -1)
        taller = jnp.concatenate([current, lower_rows], axis=1)
        right_cols = shifted(taller[:, :, :margin], "col", -1)
        extended = jnp.concatenate([taller, right_cols], axis=2)
        grad_ext, probe_grad, power = one_pass(
            extended, probe_now, amplitudes, offsets, counts, tables
        )
        rim_right = shifted(grad_ext[:, :, tile_cols:], "col", 1)
        narrowed = grad_ext[:, :, :tile_cols]
        narrowed = jnp.concatenate(
            [narrowed[:, :, :margin] + rim_right, narrowed[:, :, margin:]], axis=2
        )
        rim_lower = shifted(narrowed[:, tile_rows:, :], "row", 1)
        tile_grad = jnp.concatenate(
            [narrowed[:, :margin, :] + rim_lower, narrowed[:, margin:tile_rows, :]], axis=1
        )
        current = current + object_step * tile_grad / (probe_mean + tiny_value)
        power_old = jnp.sum(probe_now * probe_now)
        summed_grad, summed_power = lax.psum((probe_grad, power[0]), ("row", "col"))
        moved_probe = probe_now + summed_grad / (
            jnp.sum(summed_power) / (window * window) + tiny_value
        )
        power_new = jnp.sum(moved_probe * moved_probe)
        probe_now = moved_probe * jnp.sqrt(power_old / (power_new + tiny_value))
    return (current, probe_now)


def solution(mesh):
    rows, cols = mesh.shape["row"], mesh.shape["col"]

    def shards_here(*args):
        deep = Sums.chunk(rows, cols, args[1].shape[1])
        return (shards_by_kernels if deep and deep % 8 == 0 else shards)(*args)

    return jax.shard_map(
        shards_here,
        mesh=mesh,
        in_specs=(
            P(None, "row", "col"),
            P(),
            P("row", "col", None),
            P("row", "col", None, None),
            P("row", "col"),
        ),
        out_specs=(P(None, "row", "col"), P()),
        check_vma=False,
    )
```

```python
import functools
import math

import jax
import jax.numpy as jnp
import numpy as np
from jax import lax
from jax.experimental import pallas as pl
from jax.experimental.pallas import tpu as pltpu
from jax.sharding import PartitionSpec as P

MESH = pl.DeviceIdType.MESH
HALO = 128
OUTER = 2


smooth_floor = 0.5
object_step = 0.5
tiny_value = 1e-06


def shifted(value, axis, by):
    length = lax.axis_size(axis)
    pairs = [(i, i + by) for i in range(length) if 0 <= i + by < length]
    return lax.ppermute(value, axis, pairs)


def make_tables(length):
    half = length // 2
    first = np.arange(half)[:, None]
    second = np.arange(half)[None, :]
    tables = []
    for parity in range(2):
        angles = (first * (2 * second + parity) % length) * (-2.0 * math.pi / length)
        real = np.cos(angles) / math.sqrt(length)
        imag = np.sin(angles) / math.sqrt(length)
        tables.append(np.block([[real, imag], [-imag, real]]))
    tables += [tables[0].T, tables[1].T]
    stacked = np.stack(tables).astype(np.float32)
    upper = stacked.astype(jnp.bfloat16)
    lower = (stacked - upper.astype(np.float32)).astype(jnp.bfloat16)
    sorting = np.zeros((length, length), np.float32)
    sorting[np.arange(length), np.arange(length) // 2 + half * (np.arange(length) % 2)] = 1.0
    return np.concatenate([upper, lower, sorting.astype(jnp.bfloat16)[None]])


def split(value):
    upper = value.astype(jnp.bfloat16)
    lower = (value - upper.astype(jnp.float32)).astype(jnp.bfloat16)
    return upper, lower


def dot(left, right):
    return jnp.dot(left, right, preferred_element_type=jnp.float32)


def times_table(value, tables, index):
    upper, lower = split(value)
    return (
        dot(upper, tables[index]) + dot(lower, tables[index]) + dot(upper, tables[index + 4])
    )


def table_times(tables, index, value):
    upper, lower = split(value)
    return (
        dot(tables[index], upper) + dot(tables[index], lower) + dot(tables[index + 4], upper)
    )


def lanes(*parts):
    return jnp.concatenate(parts, axis=1)


def stack(*parts):
    return jnp.concatenate(parts, axis=0)


def halves_of_lanes(value):
    half = value.shape[1] // 2
    return value[:, :half], value[:, half:]


def halves_of_rows(value):
    half = value.shape[0] // 2
    return value[:half], value[half:]


def forward(real, imag, tables):
    real_l, real_r = halves_of_lanes(real)
    imag_l, imag_r = halves_of_lanes(imag)
    even = times_table(lanes(real_l + real_r, imag_l + imag_r), tables, 0)
    odd = times_table(lanes(real_l - real_r, imag_l - imag_r), tables, 1)
    even_t, even_b = halves_of_rows(even)
    odd_t, odd_b = halves_of_rows(odd)
    even_re, even_im = halves_of_lanes(even_t + even_b)
    odd_re, odd_im = halves_of_lanes(odd_t + odd_b)
    top = table_times(tables, 2, stack(lanes(even_re, odd_re), lanes(even_im, odd_im)))
    even_re, even_im = halves_of_lanes(even_t - even_b)
    odd_re, odd_im = halves_of_lanes(odd_t - odd_b)
    bottom = table_times(tables, 3, stack(lanes(even_re, odd_re), lanes(even_im, odd_im)))
    return top, bottom


def inverse(top, bottom, tables):
    top = table_times(tables, 0, top)
    bottom = table_times(tables, 1, bottom)
    upper_re, upper_im = halves_of_rows(top + bottom)
    lower_re, lower_im = halves_of_rows(top - bottom)
    even_ur, odd_ur = halves_of_lanes(upper_re)
    even_ui, odd_ui = halves_of_lanes(upper_im)
    even_lr, odd_lr = halves_of_lanes(lower_re)
    even_li, odd_li = halves_of_lanes(lower_im)
    even = times_table(stack(lanes(even_ur, even_ui), lanes(even_lr, even_li)), tables, 2)
    odd = times_table(stack(lanes(odd_ur, odd_ui), lanes(odd_lr, odd_li)), tables, 3)
    left_re, left_im = halves_of_lanes(even + odd)
    right_re, right_im = halves_of_lanes(even - odd)
    return lanes(left_re, right_re), lanes(left_im, right_im)


def sort_amplitudes(amp_ref, tables, hold, ordered):
    half = hold.shape[2] // 2
    for slot in range(amp_ref.shape[0]):
        upper, lower = split(amp_ref[slot])
        value = dot(upper, tables[8]) + dot(lower, tables[8])
        for side, part in enumerate(halves_of_lanes(value)):
            hold[slot, side] = part
            for parity in range(2):
                ordered[slot, parity, :, side * half : (side + 1) * half] = hold[
                    slot, side, pl.ds(parity, half, stride=2), :
                ]


def cut_window(slabs, part, first_row, first_col, window, margin):
    lane = lax.broadcasted_iota(jnp.int32, (window, margin), 1)
    inside = lane < margin - first_col
    turn = lax.rem(margin - first_col, margin)
    turned = [
        pltpu.roll(slabs[part, slab, pl.ds(first_row, window), :], turn, 1)
        for slab in range(slabs.shape[1])
    ]
    return lanes(*[jnp.where(inside, a, b) for a, b in zip(turned[:-1], turned[1:])])


def place_lanes(term, first_col, margin):
    window = term.shape[0]
    lane = lax.broadcasted_iota(jnp.int32, (window, margin), 1)
    inside = lane >= first_col
    turn = lax.rem(first_col, margin)
    turned = [
        pltpu.roll(term[:, at : at + margin], turn, 1) for at in range(0, term.shape[1], margin)
    ]
    empty = jnp.zeros((window, margin), term.dtype)
    return [jnp.where(inside, a, b) for a, b in zip(turned + [empty], [empty] + turned)]


def pass_over_windows(
    off_ref, cnt_ref, ext_ref, probe_ref, ordered, tables, grad_ref, pgrad_ref, slabs, padded
):
    slot_count = ordered.shape[0]
    window = probe_ref.shape[1]
    ext_rows = ext_ref.shape[1]
    margin = ext_rows - window
    for part in range(2):
        for slab in range(slabs.shape[1]):
            slabs[part, slab] = ext_ref[part, :, slab * margin : (slab + 1) * margin]
    probe_re = probe_ref[0]
    probe_im = probe_ref[1]
    power = None
    for slot in range(slot_count):
        first_row = off_ref[0, 0, slot, 0]
        first_col = off_ref[0, 0, slot, 1]
        live = (slot < cnt_ref[0, 0]).astype(jnp.float32)
        win_re = cut_window(slabs, 0, first_row, first_col, window, margin)
        win_im = cut_window(slabs, 1, first_row, first_col, window, margin)
        spectrum = forward(
            probe_re * win_re - probe_im * win_im, probe_re * win_im + probe_im * win_re, tables
        )
        replaced = []
        for parity, hat in enumerate(spectrum):
            measured = ordered[slot, parity]
            hat_re, hat_im = halves_of_rows(hat)
            ratio = measured * lax.rsqrt(hat_re * hat_re + hat_im * hat_im + smooth_floor) - 1.0
            ratio = ratio * live
            replaced.append(stack(hat_re * ratio, hat_im * ratio))
        diff_re, diff_im = inverse(*replaced, tables)
        terms = (probe_re * diff_re + probe_im * diff_im, probe_re * diff_im - probe_im * diff_re)
        for part, term in enumerate(terms):
            empty = jnp.zeros((margin, margin), jnp.float32)
            for slab, placed in enumerate(place_lanes(term, first_col, margin)):
                box = padded.at[slot, part, slab]
                box[:margin] = empty
                box[margin : margin + window] = placed
                box[margin + window :] = empty
                shown = box[pl.ds(margin - first_row, ext_rows), :]
                here = slice(slab * margin, (slab + 1) * margin)
                if slot == 0:
                    grad_ref[part, :, here] = shown
                else:
                    grad_ref[part, :, here] += shown
        probe_terms = (win_re * diff_re + win_im * diff_im, win_re * diff_im - win_im * diff_re)
        for part, term in enumerate(probe_terms):
            pgrad_ref[part] = term if slot == 0 else pgrad_ref[part] + term
        squares = jnp.sum(win_re * win_re + win_im * win_im, axis=0, keepdims=True) * live
        power = squares if power is None else power + squares
    return power


def pass_kernel(
    off_ref, cnt_ref, ext_ref, probe_ref, amp_ref, tables, grad_ref, pgrad_ref, power_ref, *scratch
):
    hold, ordered, slabs, padded = scratch
    sort_amplitudes(amp_ref, tables, hold, ordered)
    power = pass_over_windows(
        off_ref, cnt_ref, ext_ref, probe_ref, ordered, tables, grad_ref, pgrad_ref, slabs, padded
    )
    power_ref[...] = jnp.broadcast_to(power, power_ref.shape)


def pass_scratch(slots, window, ext_rows, ext_cols):
    margin = ext_rows - window
    return [
        pltpu.VMEM((slots, 2, window, window // 2), jnp.float32),
        pltpu.VMEM((slots, 2, window // 2, window), jnp.float32),
        pltpu.VMEM((2, ext_cols // margin, ext_rows, margin), jnp.float32),
        pltpu.VMEM((slots, 2, ext_cols // margin, window + 2 * margin, margin), jnp.float32),
    ]


def one_pass(extended, probe, amplitudes, offsets, counts, tables):
    slots, window = amplitudes.shape[0], probe.shape[1]
    ext_rows, ext_cols = extended.shape[1:]
    smem = pl.BlockSpec(memory_space=pltpu.SMEM)
    vmem = pl.BlockSpec(memory_space=pltpu.VMEM)
    return pl.pallas_call(
        pass_kernel,
        out_shape=(
            jax.ShapeDtypeStruct(extended.shape, jnp.float32),
            jax.ShapeDtypeStruct(probe.shape, jnp.float32),
            jax.ShapeDtypeStruct((8, window), jnp.float32),
        ),
        in_specs=[smem, smem, vmem, vmem, vmem, vmem],
        out_specs=(vmem, vmem, vmem),
        scratch_shapes=pass_scratch(slots, window, ext_rows, ext_cols),
        compiler_params=pltpu.CompilerParams(vmem_limit_bytes=40 * 2**20),
        name="window_pass",
    )(offsets, counts, extended, probe, amplitudes, tables)


def remote(src, dst, send_sem, recv_sem, **where):
    return pltpu.make_async_remote_copy(
        src_ref=src,
        dst_ref=dst,
        send_sem=send_sem,
        recv_sem=recv_sem,
        device_id=where,
        device_id_type=MESH,
    )


class Place:
    def __init__(self):
        self.rows = lax.axis_size("row")
        self.cols = lax.axis_size("col")
        self.row = lax.axis_index("row")
        self.col = lax.axis_index("col")
        self.has_up = self.row > 0
        self.has_down = self.row < self.rows - 1
        self.has_left = self.col > 0
        self.has_right = self.col < self.cols - 1
        self.up = lax.max(self.row - 1, 0)
        self.down = lax.min(self.row + 1, self.rows - 1)
        self.left = lax.max(self.col - 1, 0)
        self.right = lax.min(self.col + 1, self.cols - 1)

    def other_row(self, step):
        return lax.rem(self.row + step, self.rows)

    def other_col(self, step):
        return lax.rem(self.col + step, self.cols)

    def greet(self):
        barrier = pltpu.get_barrier_semaphore()
        for step in range(1, self.cols):
            pl.semaphore_signal(
                barrier, inc=1, device_id={"col": self.other_col(step)}, device_id_type=MESH
            )
        for step in range(1, self.rows):
            pl.semaphore_signal(
                barrier, inc=1, device_id={"row": self.other_row(step)}, device_id_type=MESH
            )

    def await_greetings(self):
        pl.semaphore_wait(pltpu.get_barrier_semaphore(), self.rows + self.cols - 2)


class Halo:
    @staticmethod
    def scratch(tile_rows, tile_cols, margin):
        return [
            pltpu.VMEM((2, margin, tile_cols), jnp.float32),
            pltpu.VMEM((2, tile_rows, margin), jnp.float32),
            pltpu.VMEM((2, margin, margin), jnp.float32),
            pltpu.SemaphoreType.DMA((3,)),
            pltpu.SemaphoreType.DMA((3,)),
        ]

    def __init__(self, place, object_ref, below, beside, corner, sent, came):
        self.place, self.object_ref = place, object_ref
        self.below, self.beside, self.corner = below, beside, corner
        margin = corner.shape[1]
        self.margin = margin
        self.from_below = remote(
            object_ref.at[:, pl.ds(0, margin), :], below, sent.at[0], came.at[0], row=place.up
        )
        self.from_beside = remote(
            object_ref.at[:, :, pl.ds(0, margin)], beside, sent.at[1], came.at[1], col=place.left
        )
        self.from_corner = remote(
            below.at[:, :, pl.ds(0, margin)], corner, sent.at[2], came.at[2], col=place.left
        )

    def start(self):
        pl.when(self.place.has_up)(self.from_below.start)
        pl.when(self.place.has_left)(self.from_beside.start)

    def finish(self, ext_ref):
        place, margin = self.place, self.margin
        _, tile_rows, tile_cols = self.object_ref.shape
        ext_ref[:, :tile_rows, :tile_cols] = self.object_ref[...]

        @pl.when(place.has_down)
        def _():
            self.from_below.wait_recv()
            pl.when(place.has_left)(self.from_corner.start)
            ext_ref[:, tile_rows:, :tile_cols] = self.below[...]

        @pl.when(jnp.logical_not(place.has_down))
        def _():
            ext_ref[:, tile_rows:, :] = jnp.zeros((2, margin, tile_cols + margin), jnp.float32)

        @pl.when(place.has_right)
        def _():
            self.from_beside.wait_recv()
            ext_ref[:, :tile_rows, tile_cols:] = self.beside[...]

            @pl.when(place.has_down)
            def _():
                self.from_corner.wait_recv()
                ext_ref[:, tile_rows:, tile_cols:] = self.corner[...]

        @pl.when(jnp.logical_not(place.has_right))
        def _():
            ext_ref[:, :, tile_cols:] = jnp.zeros((2, tile_rows + margin, margin), jnp.float32)

    def settle(self):
        place = self.place
        pl.when(place.has_up)(self.from_below.wait_send)
        pl.when(place.has_left)(self.from_beside.wait_send)
        pl.when(jnp.logical_and(place.has_left, place.has_down))(self.from_corner.wait_send)


class Rims:
    @staticmethod
    def scratch(tile_rows, tile_cols, margin):
        tall, wide = tile_rows + margin, tile_cols + margin
        return [
            pltpu.VMEM((2, tall, wide), jnp.float32),
            pltpu.VMEM((2, tall, margin), jnp.float32),
            pltpu.VMEM((2, tall, margin), jnp.float32),
            pltpu.VMEM((2, margin, tile_cols), jnp.float32),
            pltpu.VMEM((2, margin, tile_cols), jnp.float32),
            pltpu.VMEM((2, margin, margin), jnp.float32),
            pltpu.VMEM((2, margin, margin), jnp.float32),
            pltpu.SemaphoreType.DMA((6,)),
            pltpu.SemaphoreType.DMA((6,)),
        ]

    def __init__(self, place, last, grad, total, left, right, above, below, over, under, sent, came):
        self.place, self.last, self.grad, self.total = place, last, grad, total
        self.left, self.right, self.above, self.below = left, right, above, below
        self.over, self.under = over, under
        margin = over.shape[1]
        tile_rows, tile_cols = grad.shape[1] - margin, grad.shape[2] - margin
        self.sizes = margin, tile_rows, tile_cols
        first, own = pl.ds(0, margin), pl.ds(0, tile_cols)
        self.to_right = remote(
            grad.at[:, :, pl.ds(tile_cols, margin)], left, sent.at[0], came.at[0], col=place.right
        )
        self.to_left = remote(grad.at[:, :, first], right, sent.at[1], came.at[1], col=place.left)
        self.to_down = remote(
            total.at[:, pl.ds(tile_rows, margin), own], above, sent.at[2], came.at[2], row=place.down
        )
        self.to_up = remote(total.at[:, first, own], below, sent.at[3], came.at[3], row=place.up)
        self.pass_over = remote(
            above.at[:, :, first], over, sent.at[4], came.at[4], col=place.left
        )
        self.pass_under = remote(
            below.at[:, :, first], under, sent.at[5], came.at[5], col=place.left
        )

    def start(self):
        pl.when(self.place.has_right)(self.to_right.start)
        if not self.last:
            pl.when(self.place.has_left)(self.to_left.start)

    def start_rows(self):
        place, grad, total = self.place, self.grad, self.total
        margin, tile_rows, tile_cols = self.sizes
        total[...] = grad[...]

        @pl.when(place.has_left)
        def _():
            self.to_right.wait_recv()
            total[:, :, :margin] += self.left[...]

        if not self.last:

            @pl.when(place.has_right)
            def _():
                self.to_left.wait_recv()
                total[:, :, tile_cols:] += self.right[...]

        pl.when(place.has_down)(self.to_down.start)
        if not self.last:
            pl.when(place.has_up)(self.to_up.start)

    def finish(self, old_ref, new_ref, factor):
        place, total = self.place, self.total
        margin, tile_rows, tile_cols = self.sizes
        new_ref[:, margin:tile_rows, :tile_cols] = (
            old_ref[:, margin:tile_rows, :tile_cols] + factor * total[:, margin:tile_rows, :tile_cols]
        )

        @pl.when(place.has_up)
        def _():
            self.to_down.wait_recv()
            if not self.last:
                pl.when(place.has_left)(self.pass_over.start)
            new_ref[:, :margin, :tile_cols] = old_ref[:, :margin, :tile_cols] + factor * (
                total[:, :margin, :tile_cols] + self.above[...]
            )

        @pl.when(jnp.logical_not(place.has_up))
        def _():
            new_ref[:, :margin, :tile_cols] = (
                old_ref[:, :margin, :tile_cols] + factor * total[:, :margin, :tile_cols]
            )

        if self.last:
            return

        @pl.when(place.has_down)
        def _():
            self.to_up.wait_recv()
            pl.when(place.has_left)(self.pass_under.start)
            new_ref[:, tile_rows:, :tile_cols] = old_ref[:, tile_rows:, :tile_cols] + factor * (
                total[:, tile_rows:, :tile_cols] + self.below[...]
            )

        @pl.when(jnp.logical_not(place.has_down))
        def _():
            new_ref[:, tile_rows:, :] = jnp.zeros((2, margin, tile_cols + margin), jnp.float32)

        @pl.when(place.has_right)
        def _():
            new_ref[:, margin:tile_rows, tile_cols:] = (
                old_ref[:, margin:tile_rows, tile_cols:]
                + factor * total[:, margin:tile_rows, tile_cols:]
            )

            @pl.when(place.has_up)
            def _():
                self.pass_over.wait_recv()
                new_ref[:, :margin, tile_cols:] = old_ref[:, :margin, tile_cols:] + factor * (
                    total[:, :margin, tile_cols:] + self.over[...]
                )

            @pl.when(jnp.logical_not(place.has_up))
            def _():
                new_ref[:, :margin, tile_cols:] = (
                    old_ref[:, :margin, tile_cols:] + factor * total[:, :margin, tile_cols:]
                )

            @pl.when(place.has_down)
            def _():
                self.pass_under.wait_recv()
                new_ref[:, tile_rows:, tile_cols:] = old_ref[:, tile_rows:, tile_cols:] + factor * (
                    total[:, tile_rows:, tile_cols:] + self.under[...]
                )

        @pl.when(jnp.logical_not(place.has_right))
        def _():
            new_ref[:, :, tile_cols:] = jnp.zeros((2, tile_rows + margin, margin), jnp.float32)

    def settle(self):
        place = self.place
        pl.when(place.has_right)(self.to_right.wait_send)
        pl.when(place.has_down)(self.to_down.wait_send)
        if not self.last:
            pl.when(place.has_left)(self.to_left.wait_send)
            pl.when(place.has_up)(self.to_up.wait_send)
            pl.when(jnp.logical_and(place.has_left, place.has_up))(self.pass_over.wait_send)
            pl.when(jnp.logical_and(place.has_left, place.has_down))(self.pass_under.wait_send)


class Sums:
    extra = 1

    @staticmethod
    def chunk(rows, cols, window):
        return 2 * window * window // 128 // (rows * cols)

    @classmethod
    def scratch(cls, rows, cols, window):
        deep = cls.chunk(rows, cols, window)
        full = deep + cls.extra
        more_cols, more_rows = max(cols - 1, 1), rows - 1
        return [
            pltpu.VMEM((cols, rows, full, 128), jnp.float32),
            pltpu.VMEM((more_cols, rows, full, 128), jnp.float32),
            pltpu.VMEM((rows, full, 128), jnp.float32),
            pltpu.VMEM((more_rows, full, 128), jnp.float32),
            pltpu.VMEM((cols, rows, deep, 128), jnp.float32),
            pltpu.SemaphoreType.DMA((2, more_cols)),
            pltpu.SemaphoreType.DMA((2, more_rows)),
            pltpu.SemaphoreType.DMA((2, more_rows)),
            pltpu.SemaphoreType.DMA((2, more_cols, rows)),
        ]

    def __init__(self, place, whole, from_cols, part, from_rows, gathered, sems, sems2, sems3, sems4):
        self.place, self.whole, self.from_cols, self.part = place, whole, from_cols, part
        self.from_rows, self.gathered = from_rows, gathered
        self.deep = gathered.shape[2]
        self.over_cols = [
            remote(
                whole.at[place.other_col(step)],
                from_cols.at[step - 1],
                sems.at[0, step - 1],
                sems.at[1, step - 1],
                col=place.other_col(step),
            )
            for step in range(1, place.cols)
        ]
        self.over_rows = [
            remote(
                part.at[place.other_row(step)],
                from_rows.at[step - 1],
                sems2.at[0, step - 1],
                sems2.at[1, step - 1],
                row=place.other_row(step),
            )
            for step in range(1, place.rows)
        ]
        mine = gathered.at[place.col, place.row]
        self.back_rows = [
            remote(
                mine,
                mine,
                sems3.at[0, step - 1],
                sems3.at[1, step - 1],
                row=place.other_row(step),
            )
            for step in range(1, place.rows)
        ]
        self.back_cols = []
        for step in range(place.rows):
            chunk = gathered.at[place.col, place.other_row(place.rows - step)]
            self.back_cols.append(
                [
                    remote(
                        chunk,
                        chunk,
                        sems4.at[0, other - 1, step],
                        sems4.at[1, other - 1, step],
                        col=place.other_col(other),
                    )
                    for other in range(1, place.cols)
                ]
            )

    def slots(self, window):
        per = window // self.deep
        for number in range(self.place.cols * self.place.rows):
            slab, at = divmod(number, per)
            half, col = divmod(slab, window // 128)
            yield half, col * 128, at * self.deep, number // self.place.rows, number % self.place.rows

    def fill(self, pgrad_ref, power):
        window = pgrad_ref.shape[1]
        for half, lane, line, col, row in self.slots(window):
            self.whole[col, row, : self.deep] = pgrad_ref[
                half, line : line + self.deep, lane : lane + 128
            ]
        folded = sum(power[:, at : at + 128] for at in range(0, window, 128))
        first = lax.broadcasted_iota(jnp.int32, (self.extra, 128), 0) == 0
        block = jnp.where(first, jnp.broadcast_to(folded, (self.extra, 128)), 0.0)
        for col in range(self.place.cols):
            for row in range(self.place.rows):
                self.whole[col, row, self.deep :] = block

    def start(self):
        for copy in self.over_cols:
            copy.start()

    def start_rows(self):
        self.part[...] = self.whole[self.place.col]
        for step, copy in enumerate(self.over_cols):
            copy.wait_recv()
            self.part[...] += self.from_cols[step]
        for copy in self.over_rows:
            copy.start()

    def start_back(self):
        total = self.part[self.place.row]
        for step, copy in enumerate(self.over_rows):
            copy.wait_recv()
            total = total + self.from_rows[step]
        self.gathered[self.place.col, self.place.row] = total[: self.deep]
        for copy in self.back_rows + self.back_cols[0]:
            copy.start()
        return jnp.sum(total[self.deep :])

    def pass_on(self):
        for step, copy in enumerate(self.back_rows):
            copy.wait_recv()
            for other in self.back_cols[step + 1]:
                other.start()

    def finish(self, power, probe_ref, new_ref):
        window = probe_ref.shape[1]
        for copies in self.back_cols:
            for copy in copies:
                copy.wait_recv()
        old = jnp.sum(probe_ref[...] * probe_ref[...], keepdims=True)
        scale = 1.0 / (power / (window * window) + tiny_value)
        for half, lane, line, col, row in self.slots(window):
            here = (half, slice(line, line + self.deep), slice(lane, lane + 128))
            moved = probe_ref[here] + self.gathered[col, row] * scale
            new_ref[here] = moved
        moved = new_ref[...]
        new = jnp.sum(moved * moved, keepdims=True)
        new_ref[...] = moved * jnp.sqrt(old / (new + tiny_value))

    def settle(self):
        for copy in self.over_cols + self.over_rows + self.back_rows:
            copy.wait_send()
        for copies in self.back_cols:
            for copy in copies:
                copy.wait_send()


def whole_kernel(
    counts_of, off_ref, cnt_ref, object_ref, probe_ref, amp_hbm, tab_hbm, out_ref, new_ref, *scratch
):
    scratch = list(scratch)
    groups = []
    for count in counts_of:
        groups.append(scratch[:count])
        del scratch[:count]
    own, pass_refs, halo_refs, *step_refs = groups
    amp_ref, tab_ref, loads, ext_a, ext_b, probe_b, grad_ref, pgrad_ref = own
    hold, ordered, slabs, padded = pass_refs
    place = Place()
    place.greet()
    amp_load = pltpu.make_async_copy(amp_hbm, amp_ref, loads.at[0])
    tab_load = pltpu.make_async_copy(tab_hbm, tab_ref, loads.at[1])
    amp_load.start()
    tab_load.start()
    halo = Halo(place, object_ref, *halo_refs)
    place.await_greetings()
    halo.start()
    amp_load.wait()
    tab_load.wait()
    sort_amplitudes(amp_ref, tab_ref, hold, ordered)
    halo.finish(ext_a)
    exts, probes = [ext_a, ext_b], [probe_ref, probe_b]
    for step in range(OUTER):
        last = step == OUTER - 1
        ext, probe = exts[step % 2], probes[step % 2]
        power = pass_over_windows(
            off_ref, cnt_ref, ext, probe, ordered, tab_ref, grad_ref, pgrad_ref, slabs, padded
        )
        rim_refs, sum_refs = step_refs[2 * step : 2 * step + 2]
        rims = Rims(place, last, grad_ref, *rim_refs)
        sums = Sums(place, *sum_refs)
        sums.fill(pgrad_ref, power)
        if last:
            exchange(rims, sums, ext, probe, out_ref, new_ref)
        else:
            exchange(rims, sums, ext, probe, exts[1 - step % 2], probes[1 - step % 2])
    halo.settle()


def exchange(rims, sums, ext_ref, probe_ref, out_ref, new_ref):
    window = probe_ref.shape[1]
    sums.start()
    rims.start()
    sums.start_rows()
    rims.start_rows()
    power = sums.start_back()
    mean = jnp.sum(probe_ref[...] * probe_ref[...]) / (window * window)
    rims.finish(ext_ref, out_ref, object_step / (mean + tiny_value))
    sums.pass_on()
    sums.finish(power, probe_ref, new_ref)
    rims.settle()
    sums.settle()


def shards_by_kernel(object_field, probe_field, amplitudes, offsets, counts):
    tables = jnp.asarray(make_tables(probe_field.shape[1]))
    _, tile_rows, tile_cols = object_field.shape
    slots, window = amplitudes.shape[0], probe_field.shape[1]
    rows, cols = lax.axis_size("row"), lax.axis_size("col")
    extended = (2, tile_rows + HALO, tile_cols + HALO)
    own = [
        pltpu.VMEM(amplitudes.shape, jnp.float32),
        pltpu.VMEM(tables.shape, jnp.bfloat16),
        pltpu.SemaphoreType.DMA((2,)),
        pltpu.VMEM(extended, jnp.float32),
        pltpu.VMEM(extended, jnp.float32),
        pltpu.VMEM(probe_field.shape, jnp.float32),
        pltpu.VMEM(extended, jnp.float32),
        pltpu.VMEM(probe_field.shape, jnp.float32),
    ]
    groups = [own, pass_scratch(slots, window, *extended[1:]), Halo.scratch(tile_rows, tile_cols, HALO)]
    for step in range(OUTER):
        groups.append(Rims.scratch(tile_rows, tile_cols, HALO))
        groups.append(Sums.scratch(rows, cols, window))
    smem = pl.BlockSpec(memory_space=pltpu.SMEM)
    vmem = pl.BlockSpec(memory_space=pltpu.VMEM)
    anywhere = pl.BlockSpec(memory_space=pl.ANY)
    return pl.pallas_call(
        functools.partial(whole_kernel, [len(group) for group in groups]),
        out_shape=(
            jax.ShapeDtypeStruct(object_field.shape, jnp.float32),
            jax.ShapeDtypeStruct(probe_field.shape, jnp.float32),
        ),
        in_specs=[smem, smem, vmem, vmem, anywhere, anywhere],
        out_specs=(vmem, vmem),
        scratch_shapes=sum(groups, []),
        compiler_params=pltpu.CompilerParams(
            collective_id=0, has_side_effects=True, vmem_limit_bytes=50 * 2**20
        ),
        name="refinement",
    )(offsets, counts, object_field, probe_field, amplitudes, tables)


def shards(object_field, probe_field, amplitudes, offsets, counts):
    tile_rows = object_field.shape[1]
    tile_cols = object_field.shape[2]
    window = probe_field.shape[1]
    margin = HALO
    tables = jnp.asarray(make_tables(window))
    current = object_field
    probe_now = probe_field
    for outer_step in range(OUTER):
        probe_mean = jnp.sum(probe_now * probe_now) / (window * window)
        lower_rows = shifted(current[:, :margin, :], "row", -1)
        taller = jnp.concatenate([current, lower_rows], axis=1)
        right_cols = shifted(taller[:, :, :margin], "col", -1)
        extended = jnp.concatenate([taller, right_cols], axis=2)
        grad_ext, probe_grad, power = one_pass(
            extended, probe_now, amplitudes, offsets, counts, tables
        )
        rim_right = shifted(grad_ext[:, :, tile_cols:], "col", 1)
        narrowed = grad_ext[:, :, :tile_cols]
        narrowed = jnp.concatenate(
            [narrowed[:, :, :margin] + rim_right, narrowed[:, :, margin:]], axis=2
        )
        rim_lower = shifted(narrowed[:, tile_rows:, :], "row", 1)
        tile_grad = jnp.concatenate(
            [narrowed[:, :margin, :] + rim_lower, narrowed[:, margin:tile_rows, :]], axis=1
        )
        current = current + object_step * tile_grad / (probe_mean + tiny_value)
        power_old = jnp.sum(probe_now * probe_now)
        summed_grad, summed_power = lax.psum((probe_grad, power[0]), ("row", "col"))
        moved_probe = probe_now + summed_grad / (
            jnp.sum(summed_power) / (window * window) + tiny_value
        )
        power_new = jnp.sum(moved_probe * moved_probe)
        probe_now = moved_probe * jnp.sqrt(power_old / (power_new + tiny_value))
    return (current, probe_now)


def solution(mesh):
    rows, cols = mesh.shape["row"], mesh.shape["col"]

    def shards_here(*args):
        deep = Sums.chunk(rows, cols, args[1].shape[1])
        return (shards_by_kernel if deep and deep % 8 == 0 else shards)(*args)

    return jax.shard_map(
        shards_here,
        mesh=mesh,
        in_specs=(
            P(None, "row", "col"),
            P(),
            P("row", "col", None),
            P("row", "col", None, None),
            P("row", "col"),
        ),
        out_specs=(P(None, "row", "col"), P()),
        check_vma=False,
    )
```

```python
import functools
import math

import jax
import jax.numpy as jnp
import numpy as np
from jax import lax
from jax.experimental import pallas as pl
from jax.experimental.pallas import tpu as pltpu
from jax.sharding import PartitionSpec as P

MESH = pl.DeviceIdType.MESH
HALO = 128
OUTER = 2


smooth_floor = 0.5
object_step = 0.5
tiny_value = 1e-06


def shifted(value, axis, by):
    length = lax.axis_size(axis)
    pairs = [(i, i + by) for i in range(length) if 0 <= i + by < length]
    return lax.ppermute(value, axis, pairs)


def make_tables(length):
    half = length // 2
    first = np.arange(half)[:, None]
    second = np.arange(half)[None, :]
    tables = []
    for parity in range(2):
        angles = (first * (2 * second + parity) % length) * (-2.0 * math.pi / length)
        real = np.cos(angles) / math.sqrt(length)
        imag = np.sin(angles) / math.sqrt(length)
        tables.append(np.block([[real, imag], [-imag, real]]))
    tables += [tables[0].T, tables[1].T]
    stacked = np.stack(tables).astype(np.float32)
    upper = stacked.astype(jnp.bfloat16)
    lower = (stacked - upper.astype(np.float32)).astype(jnp.bfloat16)
    sorting = np.zeros((length, length), np.float32)
    sorting[np.arange(length), np.arange(length) // 2 + half * (np.arange(length) % 2)] = 1.0
    return np.concatenate([upper, lower, sorting.astype(jnp.bfloat16)[None]])


def split(value):
    upper = value.astype(jnp.bfloat16)
    lower = (value - upper.astype(jnp.float32)).astype(jnp.bfloat16)
    return upper, lower


def dot(left, right):
    return jnp.dot(left, right, preferred_element_type=jnp.float32)


def times_table(value, tables, index):
    upper, lower = split(value)
    return (
        dot(upper, tables[index]) + dot(lower, tables[index]) + dot(upper, tables[index + 4])
    )


def table_times(tables, index, value):
    upper, lower = split(value)
    return (
        dot(tables[index], upper) + dot(tables[index], lower) + dot(tables[index + 4], upper)
    )


def lanes(*parts):
    return jnp.concatenate(parts, axis=1)


def stack(*parts):
    return jnp.concatenate(parts, axis=0)


def halves_of_lanes(value):
    half = value.shape[1] // 2
    return value[:, :half], value[:, half:]


def halves_of_rows(value):
    half = value.shape[0] // 2
    return value[:half], value[half:]


def forward(real, imag, tables):
    real_l, real_r = halves_of_lanes(real)
    imag_l, imag_r = halves_of_lanes(imag)
    even = times_table(lanes(real_l + real_r, imag_l + imag_r), tables, 0)
    odd = times_table(lanes(real_l - real_r, imag_l - imag_r), tables, 1)
    even_t, even_b = halves_of_rows(even)
    odd_t, odd_b = halves_of_rows(odd)
    even_re, even_im = halves_of_lanes(even_t + even_b)
    odd_re, odd_im = halves_of_lanes(odd_t + odd_b)
    top = table_times(tables, 2, stack(lanes(even_re, odd_re), lanes(even_im, odd_im)))
    even_re, even_im = halves_of_lanes(even_t - even_b)
    odd_re, odd_im = halves_of_lanes(odd_t - odd_b)
    bottom = table_times(tables, 3, stack(lanes(even_re, odd_re), lanes(even_im, odd_im)))
    return top, bottom


def inverse(top, bottom, tables):
    top = table_times(tables, 0, top)
    bottom = table_times(tables, 1, bottom)
    upper_re, upper_im = halves_of_rows(top + bottom)
    lower_re, lower_im = halves_of_rows(top - bottom)
    even_ur, odd_ur = halves_of_lanes(upper_re)
    even_ui, odd_ui = halves_of_lanes(upper_im)
    even_lr, odd_lr = halves_of_lanes(lower_re)
    even_li, odd_li = halves_of_lanes(lower_im)
    even = times_table(stack(lanes(even_ur, even_ui), lanes(even_lr, even_li)), tables, 2)
    odd = times_table(stack(lanes(odd_ur, odd_ui), lanes(odd_lr, odd_li)), tables, 3)
    left_re, left_im = halves_of_lanes(even + odd)
    right_re, right_im = halves_of_lanes(even - odd)
    return lanes(left_re, right_re), lanes(left_im, right_im)


def sort_amplitudes(amp_ref, tables, hold, ordered):
    half = hold.shape[2] // 2
    for slot in range(amp_ref.shape[0]):
        upper, lower = split(amp_ref[slot])
        value = dot(upper, tables[8]) + dot(lower, tables[8])
        for side, part in enumerate(halves_of_lanes(value)):
            hold[slot, side] = part
            for parity in range(2):
                ordered[slot, parity, :, side * half : (side + 1) * half] = hold[
                    slot, side, pl.ds(parity, half, stride=2), :
                ]


def cut_window(slabs, part, first_row, first_col, window, margin):
    lane = lax.broadcasted_iota(jnp.int32, (window, margin), 1)
    inside = lane < margin - first_col
    turn = lax.rem(margin - first_col, margin)
    turned = [
        pltpu.roll(slabs[part, slab, pl.ds(first_row, window), :], turn, 1)
        for slab in range(slabs.shape[1])
    ]
    return lanes(*[jnp.where(inside, a, b) for a, b in zip(turned[:-1], turned[1:])])


def place_lanes(term, first_col, margin):
    window = term.shape[0]
    lane = lax.broadcasted_iota(jnp.int32, (window, margin), 1)
    inside = lane >= first_col
    turn = lax.rem(first_col, margin)
    turned = [
        pltpu.roll(term[:, at : at + margin], turn, 1) for at in range(0, term.shape[1], margin)
    ]
    empty = jnp.zeros((window, margin), term.dtype)
    return [jnp.where(inside, a, b) for a, b in zip(turned + [empty], [empty] + turned)]


def pass_over_windows(
    off_ref, cnt_ref, ext_ref, probe_ref, ordered, tables, grad_ref, pgrad_ref, slabs, padded
):
    slot_count = ordered.shape[0]
    window = probe_ref.shape[1]
    ext_rows = ext_ref.shape[1]
    margin = ext_rows - window
    for part in range(2):
        for slab in range(slabs.shape[1]):
            slabs[part, slab] = ext_ref[part, :, slab * margin : (slab + 1) * margin]
    probe_re = probe_ref[0]
    probe_im = probe_ref[1]
    power = None
    for slot in range(slot_count):
        first_row = off_ref[0, 0, slot, 0]
        first_col = off_ref[0, 0, slot, 1]
        live = (slot < cnt_ref[0, 0]).astype(jnp.float32)
        win_re = cut_window(slabs, 0, first_row, first_col, window, margin)
        win_im = cut_window(slabs, 1, first_row, first_col, window, margin)
        spectrum = forward(
            probe_re * win_re - probe_im * win_im, probe_re * win_im + probe_im * win_re, tables
        )
        replaced = []
        for parity, hat in enumerate(spectrum):
            measured = ordered[slot, parity]
            hat_re, hat_im = halves_of_rows(hat)
            ratio = measured * lax.rsqrt(hat_re * hat_re + hat_im * hat_im + smooth_floor) - 1.0
            ratio = ratio * live
            replaced.append(stack(hat_re * ratio, hat_im * ratio))
        diff_re, diff_im = inverse(*replaced, tables)
        terms = (probe_re * diff_re + probe_im * diff_im, probe_re * diff_im - probe_im * diff_re)
        for part, term in enumerate(terms):
            empty = jnp.zeros((margin, margin), jnp.float32)
            for slab, placed in enumerate(place_lanes(term, first_col, margin)):
                box = padded.at[slot, part, slab]
                box[:margin] = empty
                box[margin : margin + window] = placed
                box[margin + window :] = empty
                shown = box[pl.ds(margin - first_row, ext_rows), :]
                here = slice(slab * margin, (slab + 1) * margin)
                if slot == 0:
                    grad_ref[part, :, here] = shown
                else:
                    grad_ref[part, :, here] += shown
        probe_terms = (win_re * diff_re + win_im * diff_im, win_re * diff_im - win_im * diff_re)
        for part, term in enumerate(probe_terms):
            pgrad_ref[part] = term if slot == 0 else pgrad_ref[part] + term
        squares = jnp.sum(win_re * win_re + win_im * win_im, axis=0, keepdims=True) * live
        power = squares if power is None else power + squares
    return power


def pass_kernel(
    off_ref, cnt_ref, ext_ref, probe_ref, amp_ref, tables, grad_ref, pgrad_ref, power_ref, *scratch
):
    hold, ordered, slabs, padded = scratch
    sort_amplitudes(amp_ref, tables, hold, ordered)
    power = pass_over_windows(
        off_ref, cnt_ref, ext_ref, probe_ref, ordered, tables, grad_ref, pgrad_ref, slabs, padded
    )
    power_ref[...] = jnp.broadcast_to(power, power_ref.shape)


def pass_scratch(slots, window, ext_rows, ext_cols):
    margin = ext_rows - window
    return [
        pltpu.VMEM((slots, 2, window, window // 2), jnp.float32),
        pltpu.VMEM((slots, 2, window // 2, window), jnp.float32),
        pltpu.VMEM((2, ext_cols // margin, ext_rows, margin), jnp.float32),
        pltpu.VMEM((slots, 2, ext_cols // margin, window + 2 * margin, margin), jnp.float32),
    ]


def one_pass(extended, probe, amplitudes, offsets, counts, tables):
    slots, window = amplitudes.shape[0], probe.shape[1]
    ext_rows, ext_cols = extended.shape[1:]
    smem = pl.BlockSpec(memory_space=pltpu.SMEM)
    vmem = pl.BlockSpec(memory_space=pltpu.VMEM)
    return pl.pallas_call(
        pass_kernel,
        out_shape=(
            jax.ShapeDtypeStruct(extended.shape, jnp.float32),
            jax.ShapeDtypeStruct(probe.shape, jnp.float32),
            jax.ShapeDtypeStruct((8, window), jnp.float32),
        ),
        in_specs=[smem, smem, vmem, vmem, vmem, vmem],
        out_specs=(vmem, vmem, vmem),
        scratch_shapes=pass_scratch(slots, window, ext_rows, ext_cols),
        compiler_params=pltpu.CompilerParams(vmem_limit_bytes=40 * 2**20),
        name="window_pass",
    )(offsets, counts, extended, probe, amplitudes, tables)


def remote(src, dst, send_sem, recv_sem, **where):
    return pltpu.make_async_remote_copy(
        src_ref=src,
        dst_ref=dst,
        send_sem=send_sem,
        recv_sem=recv_sem,
        device_id=where,
        device_id_type=MESH,
    )


class Place:
    def __init__(self):
        self.rows = lax.axis_size("row")
        self.cols = lax.axis_size("col")
        self.row = lax.axis_index("row")
        self.col = lax.axis_index("col")
        self.has_up = self.row > 0
        self.has_down = self.row < self.rows - 1
        self.has_left = self.col > 0
        self.has_right = self.col < self.cols - 1
        self.up = lax.max(self.row - 1, 0)
        self.down = lax.min(self.row + 1, self.rows - 1)
        self.left = lax.max(self.col - 1, 0)
        self.right = lax.min(self.col + 1, self.cols - 1)

    def other_row(self, step):
        return lax.rem(self.row + step, self.rows)

    def other_col(self, step):
        return lax.rem(self.col + step, self.cols)

    def greet(self):
        barrier = pltpu.get_barrier_semaphore()
        for step in range(1, self.cols):
            pl.semaphore_signal(
                barrier, inc=1, device_id={"col": self.other_col(step)}, device_id_type=MESH
            )
        for step in range(1, self.rows):
            pl.semaphore_signal(
                barrier, inc=1, device_id={"row": self.other_row(step)}, device_id_type=MESH
            )

    def await_greetings(self):
        pl.semaphore_wait(pltpu.get_barrier_semaphore(), self.rows + self.cols - 2)


class Halo:
    @staticmethod
    def scratch(tile_rows, tile_cols, margin):
        return [
            pltpu.VMEM((2, margin, tile_cols), jnp.float32),
            pltpu.VMEM((2, tile_rows, margin), jnp.float32),
            pltpu.VMEM((2, margin, margin), jnp.float32),
            pltpu.SemaphoreType.DMA((3,)),
            pltpu.SemaphoreType.DMA((3,)),
        ]

    def __init__(self, place, object_ref, below, beside, corner, sent, came):
        self.place, self.object_ref = place, object_ref
        self.below, self.beside, self.corner = below, beside, corner
        margin = corner.shape[1]
        self.margin = margin
        self.from_below = remote(
            object_ref.at[:, pl.ds(0, margin), :], below, sent.at[0], came.at[0], row=place.up
        )
        self.from_beside = remote(
            object_ref.at[:, :, pl.ds(0, margin)], beside, sent.at[1], came.at[1], col=place.left
        )
        self.from_corner = remote(
            below.at[:, :, pl.ds(0, margin)], corner, sent.at[2], came.at[2], col=place.left
        )

    def start(self):
        pl.when(self.place.has_up)(self.from_below.start)
        pl.when(self.place.has_left)(self.from_beside.start)

    def finish(self, ext_ref):
        place, margin = self.place, self.margin
        _, tile_rows, tile_cols = self.object_ref.shape
        ext_ref[:, :tile_rows, :tile_cols] = self.object_ref[...]

        @pl.when(place.has_down)
        def _():
            self.from_below.wait_recv()
            pl.when(place.has_left)(self.from_corner.start)
            ext_ref[:, tile_rows:, :tile_cols] = self.below[...]

        @pl.when(jnp.logical_not(place.has_down))
        def _():
            ext_ref[:, tile_rows:, :] = jnp.zeros((2, margin, tile_cols + margin), jnp.float32)

        @pl.when(place.has_right)
        def _():
            self.from_beside.wait_recv()
            ext_ref[:, :tile_rows, tile_cols:] = self.beside[...]

            @pl.when(place.has_down)
            def _():
                self.from_corner.wait_recv()
                ext_ref[:, tile_rows:, tile_cols:] = self.corner[...]

        @pl.when(jnp.logical_not(place.has_right))
        def _():
            ext_ref[:, :, tile_cols:] = jnp.zeros((2, tile_rows + margin, margin), jnp.float32)

    def settle(self):
        place = self.place
        pl.when(place.has_up)(self.from_below.wait_send)
        pl.when(place.has_left)(self.from_beside.wait_send)
        pl.when(jnp.logical_and(place.has_left, place.has_down))(self.from_corner.wait_send)


class Rims:
    @staticmethod
    def scratch(tile_rows, tile_cols, margin):
        tall, wide = tile_rows + margin, tile_cols + margin
        return [
            pltpu.VMEM((2, tall, wide), jnp.float32),
            pltpu.VMEM((2, tall, margin), jnp.float32),
            pltpu.VMEM((2, tall, margin), jnp.float32),
            pltpu.VMEM((2, margin, tile_cols), jnp.float32),
            pltpu.VMEM((2, margin, tile_cols), jnp.float32),
            pltpu.VMEM((2, margin, margin), jnp.float32),
            pltpu.VMEM((2, margin, margin), jnp.float32),
            pltpu.SemaphoreType.DMA((6,)),
            pltpu.SemaphoreType.DMA((6,)),
        ]

    def __init__(self, place, last, grad, total, left, right, above, below, over, under, sent, came):
        self.place, self.last, self.grad, self.total = place, last, grad, total
        self.left, self.right, self.above, self.below = left, right, above, below
        self.over, self.under = over, under
        margin = over.shape[1]
        tile_rows, tile_cols = grad.shape[1] - margin, grad.shape[2] - margin
        self.sizes = margin, tile_rows, tile_cols
        first, own = pl.ds(0, margin), pl.ds(0, tile_cols)
        self.to_right = remote(
            grad.at[:, :, pl.ds(tile_cols, margin)], left, sent.at[0], came.at[0], col=place.right
        )
        self.to_left = remote(grad.at[:, :, first], right, sent.at[1], came.at[1], col=place.left)
        self.to_down = remote(
            total.at[:, pl.ds(tile_rows, margin), own], above, sent.at[2], came.at[2], row=place.down
        )
        self.to_up = remote(total.at[:, first, own], below, sent.at[3], came.at[3], row=place.up)
        self.pass_over = remote(
            above.at[:, :, first], over, sent.at[4], came.at[4], col=place.left
        )
        self.pass_under = remote(
            below.at[:, :, first], under, sent.at[5], came.at[5], col=place.left
        )

    def start(self):
        pl.when(self.place.has_right)(self.to_right.start)
        if not self.last:
            pl.when(self.place.has_left)(self.to_left.start)

    def start_rows(self):
        place, grad, total = self.place, self.grad, self.total
        margin, tile_rows, tile_cols = self.sizes
        total[...] = grad[...]

        @pl.when(place.has_left)
        def _():
            self.to_right.wait_recv()
            total[:, :, :margin] += self.left[...]

        if not self.last:

            @pl.when(place.has_right)
            def _():
                self.to_left.wait_recv()
                total[:, :, tile_cols:] += self.right[...]

        pl.when(place.has_down)(self.to_down.start)
        if not self.last:
            pl.when(place.has_up)(self.to_up.start)

    def finish(self, old_ref, new_ref, factor):
        place, total = self.place, self.total
        margin, tile_rows, tile_cols = self.sizes
        new_ref[:, margin:tile_rows, :tile_cols] = (
            old_ref[:, margin:tile_rows, :tile_cols] + factor * total[:, margin:tile_rows, :tile_cols]
        )

        @pl.when(place.has_up)
        def _():
            self.to_down.wait_recv()
            if not self.last:
                pl.when(place.has_left)(self.pass_over.start)
            new_ref[:, :margin, :tile_cols] = old_ref[:, :margin, :tile_cols] + factor * (
                total[:, :margin, :tile_cols] + self.above[...]
            )

        @pl.when(jnp.logical_not(place.has_up))
        def _():
            new_ref[:, :margin, :tile_cols] = (
                old_ref[:, :margin, :tile_cols] + factor * total[:, :margin, :tile_cols]
            )

        if self.last:
            return

        @pl.when(place.has_down)
        def _():
            self.to_up.wait_recv()
            pl.when(place.has_left)(self.pass_under.start)
            new_ref[:, tile_rows:, :tile_cols] = old_ref[:, tile_rows:, :tile_cols] + factor * (
                total[:, tile_rows:, :tile_cols] + self.below[...]
            )

        @pl.when(jnp.logical_not(place.has_down))
        def _():
            new_ref[:, tile_rows:, :] = jnp.zeros((2, margin, tile_cols + margin), jnp.float32)

        @pl.when(place.has_right)
        def _():
            new_ref[:, margin:tile_rows, tile_cols:] = (
                old_ref[:, margin:tile_rows, tile_cols:]
                + factor * total[:, margin:tile_rows, tile_cols:]
            )

            @pl.when(place.has_up)
            def _():
                self.pass_over.wait_recv()
                new_ref[:, :margin, tile_cols:] = old_ref[:, :margin, tile_cols:] + factor * (
                    total[:, :margin, tile_cols:] + self.over[...]
                )

            @pl.when(jnp.logical_not(place.has_up))
            def _():
                new_ref[:, :margin, tile_cols:] = (
                    old_ref[:, :margin, tile_cols:] + factor * total[:, :margin, tile_cols:]
                )

            @pl.when(place.has_down)
            def _():
                self.pass_under.wait_recv()
                new_ref[:, tile_rows:, tile_cols:] = old_ref[:, tile_rows:, tile_cols:] + factor * (
                    total[:, tile_rows:, tile_cols:] + self.under[...]
                )

        @pl.when(jnp.logical_not(place.has_right))
        def _():
            new_ref[:, :, tile_cols:] = jnp.zeros((2, tile_rows + margin, margin), jnp.float32)

    def settle(self):
        place = self.place
        pl.when(place.has_right)(self.to_right.wait_send)
        pl.when(place.has_down)(self.to_down.wait_send)
        if not self.last:
            pl.when(place.has_left)(self.to_left.wait_send)
            pl.when(place.has_up)(self.to_up.wait_send)
            pl.when(jnp.logical_and(place.has_left, place.has_up))(self.pass_over.wait_send)
            pl.when(jnp.logical_and(place.has_left, place.has_down))(self.pass_under.wait_send)


class Sums:
    extra = 1

    @staticmethod
    def chunk(rows, cols, window):
        return 2 * window * window // 128 // (rows * cols)

    @staticmethod
    def group(rows):
        return max(size for size in range(1, rows + 1) if rows % size == 0 and size * size <= rows)

    @classmethod
    def scratch(cls, rows, cols, window):
        deep = cls.chunk(rows, cols, window)
        full = deep + cls.extra
        near = cls.group(rows)
        far = rows // near
        more_cols, more_near, more_far = (max(size - 1, 1) for size in (cols, near, far))
        return [
            pltpu.VMEM((cols, near, far, full, 128), jnp.float32),
            pltpu.VMEM((more_cols, near, far, full, 128), jnp.float32),
            pltpu.VMEM((near, far, full, 128), jnp.float32),
            pltpu.VMEM((more_near, far, full, 128), jnp.float32),
            pltpu.VMEM((far, full, 128), jnp.float32),
            pltpu.VMEM((more_far, full, 128), jnp.float32),
            pltpu.VMEM((cols, near, far, deep, 128), jnp.float32),
            pltpu.SemaphoreType.DMA((2, more_cols)),
            pltpu.SemaphoreType.DMA((2, 2, more_near)),
            pltpu.SemaphoreType.DMA((2, 2, more_far)),
            pltpu.SemaphoreType.DMA((2, more_cols, near)),
        ]

    def __init__(
        self, place, whole, from_cols, part, from_near, less, from_far, gathered, sems, sems2, sems3, sems4
    ):
        self.place, self.whole, self.from_cols, self.part = place, whole, from_cols, part
        self.from_near, self.less, self.from_far, self.gathered = from_near, less, from_far, gathered
        _, self.near, self.far, self.deep, _ = gathered.shape
        near, far = self.near, self.far
        self.at_far, self.at_near = place.row // near, lax.rem(place.row, near)

        def other_near(step):
            return lax.rem(self.at_near + step, near)

        def other_far(step):
            return lax.rem(self.at_far + step, far)

        self.over_cols = [
            remote(
                whole.at[place.other_col(step)],
                from_cols.at[step - 1],
                sems.at[0, step - 1],
                sems.at[1, step - 1],
                col=place.other_col(step),
            )
            for step in range(1, place.cols)
        ]
        self.over_near = [
            remote(
                part.at[other_near(step)],
                from_near.at[step - 1],
                sems2.at[0, 0, step - 1],
                sems2.at[0, 1, step - 1],
                row=self.at_far * near + other_near(step),
            )
            for step in range(1, near)
        ]
        self.over_far = [
            remote(
                less.at[other_far(step)],
                from_far.at[step - 1],
                sems3.at[0, 0, step - 1],
                sems3.at[0, 1, step - 1],
                row=other_far(step) * near + self.at_near,
            )
            for step in range(1, far)
        ]
        mine = gathered.at[place.col, self.at_near, self.at_far]
        self.back_far = [
            remote(
                mine,
                mine,
                sems3.at[1, 0, step - 1],
                sems3.at[1, 1, step - 1],
                row=other_far(step) * near + self.at_near,
            )
            for step in range(1, far)
        ]
        block = gathered.at[place.col, self.at_near]
        self.back_near = [
            remote(
                block,
                block,
                sems2.at[1, 0, step - 1],
                sems2.at[1, 1, step - 1],
                row=self.at_far * near + other_near(step),
            )
            for step in range(1, near)
        ]
        self.back_cols = []
        for step in range(near):
            block = gathered.at[place.col, other_near(near - step)]
            self.back_cols.append(
                [
                    remote(
                        block,
                        block,
                        sems4.at[0, other - 1, step],
                        sems4.at[1, other - 1, step],
                        col=place.other_col(other),
                    )
                    for other in range(1, place.cols)
                ]
            )

    def slots(self, window):
        per = window // self.deep
        for number in range(self.place.cols * self.place.rows):
            slab, at = divmod(number, per)
            half, side = divmod(slab, window // 128)
            here = (
                half,
                slice(at * self.deep, (at + 1) * self.deep),
                slice(side * 128, (side + 1) * 128),
            )
            rest, far = divmod(number, self.far)
            yield here, (rest // self.near, rest % self.near, far)

    def fill(self, pgrad_ref, power):
        window = pgrad_ref.shape[1]
        folded = sum(power[:, at : at + 128] for at in range(0, window, 128))
        for here, (col, near, far) in self.slots(window):
            self.whole[col, near, far, : self.deep] = pgrad_ref[here]
            self.whole[col, near, far, self.deep :] = folded

    def start(self):
        for copy in self.over_cols:
            copy.start()

    def start_near(self):
        self.part[...] = self.whole[self.place.col]
        for step, copy in enumerate(self.over_cols):
            copy.wait_recv()
            self.part[...] += self.from_cols[step]
        for copy in self.over_near:
            copy.start()

    def start_far(self):
        total = self.part[self.at_near]
        for step, copy in enumerate(self.over_near):
            copy.wait_recv()
            total = total + self.from_near[step]
        self.less[...] = total
        for copy in self.over_far:
            copy.start()

    def start_back(self):
        total = self.less[self.at_far]
        for step, copy in enumerate(self.over_far):
            copy.wait_recv()
            total = total + self.from_far[step]
        self.gathered[self.place.col, self.at_near, self.at_far] = total[: self.deep]
        for copy in self.back_far:
            copy.start()
        return jnp.sum(total[self.deep :])

    def start_back_near(self):
        for copy in self.back_far:
            copy.wait_recv()
        for copy in self.back_near + self.back_cols[0]:
            copy.start()

    def pass_on(self):
        for step, copy in enumerate(self.back_near):
            copy.wait_recv()
            for other in self.back_cols[step + 1]:
                other.start()

    def finish(self, power, probe_ref, new_ref):
        window = probe_ref.shape[1]
        for copies in self.back_cols:
            for copy in copies:
                copy.wait_recv()
        old = jnp.sum(probe_ref[...] * probe_ref[...], keepdims=True)
        scale = 1.0 / (power / (window * window) + tiny_value)
        for here, (col, near, far) in self.slots(window):
            new_ref[here] = probe_ref[here] + self.gathered[col, near, far] * scale
        moved = new_ref[...]
        new = jnp.sum(moved * moved, keepdims=True)
        new_ref[...] = moved * jnp.sqrt(old / (new + tiny_value))

    def settle(self):
        copies = self.over_cols + self.over_near + self.over_far + self.back_far + self.back_near
        for copy in copies + sum(self.back_cols, []):
            copy.wait_send()


def whole_kernel(
    counts_of, off_ref, cnt_ref, object_hbm, probe_hbm, amp_hbm, tab_hbm, out_ref, new_ref, *scratch
):
    scratch = list(scratch)
    groups = []
    for count in counts_of:
        groups.append(scratch[:count])
        del scratch[:count]
    own, pass_refs, halo_refs, *step_refs = groups
    object_ref, probe_ref, amp_ref, tab_ref, loads, ext_a, ext_b, probe_b, grad_ref, pgrad_ref = own
    hold, ordered, slabs, padded = pass_refs
    place = Place()
    place.greet()
    pairs = (
        (object_hbm, object_ref),
        (tab_hbm, tab_ref),
        (amp_hbm, amp_ref),
        (probe_hbm, probe_ref),
    )
    copies = [pltpu.make_async_copy(*pair, loads.at[at]) for at, pair in enumerate(pairs)]
    for copy in copies:
        copy.start()
    halo = Halo(place, object_ref, *halo_refs)
    place.await_greetings()
    copies[0].wait()
    halo.start()
    for copy in copies[1:]:
        copy.wait()
    sort_amplitudes(amp_ref, tab_ref, hold, ordered)
    halo.finish(ext_a)
    exts, probes = [ext_a, ext_b], [probe_ref, probe_b]
    for step in range(OUTER):
        last = step == OUTER - 1
        ext, probe = exts[step % 2], probes[step % 2]
        power = pass_over_windows(
            off_ref, cnt_ref, ext, probe, ordered, tab_ref, grad_ref, pgrad_ref, slabs, padded
        )
        rim_refs, sum_refs = step_refs[2 * step : 2 * step + 2]
        rims = Rims(place, last, grad_ref, *rim_refs)
        sums = Sums(place, *sum_refs)
        sums.fill(pgrad_ref, power)
        if last:
            exchange(rims, sums, ext, probe, out_ref, new_ref)
        else:
            exchange(rims, sums, ext, probe, exts[1 - step % 2], probes[1 - step % 2])
    halo.settle()


def exchange(rims, sums, ext_ref, probe_ref, out_ref, new_ref):
    window = probe_ref.shape[1]
    sums.start()
    rims.start()
    sums.start_near()
    sums.start_far()
    rims.start_rows()
    power = sums.start_back()
    sums.start_back_near()
    mean = jnp.sum(probe_ref[...] * probe_ref[...]) / (window * window)
    rims.finish(ext_ref, out_ref, object_step / (mean + tiny_value))
    sums.pass_on()
    sums.finish(power, probe_ref, new_ref)
    rims.settle()
    sums.settle()


def shards_by_kernel(object_field, probe_field, amplitudes, offsets, counts):
    tables = jnp.asarray(make_tables(probe_field.shape[1]))
    _, tile_rows, tile_cols = object_field.shape
    slots, window = amplitudes.shape[0], probe_field.shape[1]
    rows, cols = lax.axis_size("row"), lax.axis_size("col")
    extended = (2, tile_rows + HALO, tile_cols + HALO)
    own = [
        pltpu.VMEM(object_field.shape, jnp.float32),
        pltpu.VMEM(probe_field.shape, jnp.float32),
        pltpu.VMEM(amplitudes.shape, jnp.float32),
        pltpu.VMEM(tables.shape, jnp.bfloat16),
        pltpu.SemaphoreType.DMA((4,)),
        pltpu.VMEM(extended, jnp.float32),
        pltpu.VMEM(extended, jnp.float32),
        pltpu.VMEM(probe_field.shape, jnp.float32),
        pltpu.VMEM(extended, jnp.float32),
        pltpu.VMEM(probe_field.shape, jnp.float32),
    ]
    groups = [own, pass_scratch(slots, window, *extended[1:]), Halo.scratch(tile_rows, tile_cols, HALO)]
    for step in range(OUTER):
        groups.append(Rims.scratch(tile_rows, tile_cols, HALO))
        groups.append(Sums.scratch(rows, cols, window))
    smem = pl.BlockSpec(memory_space=pltpu.SMEM)
    vmem = pl.BlockSpec(memory_space=pltpu.VMEM)
    anywhere = pl.BlockSpec(memory_space=pl.ANY)
    return pl.pallas_call(
        functools.partial(whole_kernel, [len(group) for group in groups]),
        out_shape=(
            jax.ShapeDtypeStruct(object_field.shape, jnp.float32),
            jax.ShapeDtypeStruct(probe_field.shape, jnp.float32),
        ),
        in_specs=[smem, smem, anywhere, anywhere, anywhere, anywhere],
        out_specs=(vmem, vmem),
        scratch_shapes=sum(groups, []),
        compiler_params=pltpu.CompilerParams(
            collective_id=0, has_side_effects=True, vmem_limit_bytes=60 * 2**20
        ),
        name="refinement",
    )(offsets, counts, object_field, probe_field, amplitudes, tables)


def shards(object_field, probe_field, amplitudes, offsets, counts):
    tile_rows = object_field.shape[1]
    tile_cols = object_field.shape[2]
    window = probe_field.shape[1]
    margin = HALO
    tables = jnp.asarray(make_tables(window))
    current = object_field
    probe_now = probe_field
    for outer_step in range(OUTER):
        probe_mean = jnp.sum(probe_now * probe_now) / (window * window)
        lower_rows = shifted(current[:, :margin, :], "row", -1)
        taller = jnp.concatenate([current, lower_rows], axis=1)
        right_cols = shifted(taller[:, :, :margin], "col", -1)
        extended = jnp.concatenate([taller, right_cols], axis=2)
        grad_ext, probe_grad, power = one_pass(
            extended, probe_now, amplitudes, offsets, counts, tables
        )
        rim_right = shifted(grad_ext[:, :, tile_cols:], "col", 1)
        narrowed = grad_ext[:, :, :tile_cols]
        narrowed = jnp.concatenate(
            [narrowed[:, :, :margin] + rim_right, narrowed[:, :, margin:]], axis=2
        )
        rim_lower = shifted(narrowed[:, tile_rows:, :], "row", 1)
        tile_grad = jnp.concatenate(
            [narrowed[:, :margin, :] + rim_lower, narrowed[:, margin:tile_rows, :]], axis=1
        )
        current = current + object_step * tile_grad / (probe_mean + tiny_value)
        power_old = jnp.sum(probe_now * probe_now)
        summed_grad, summed_power = lax.psum((probe_grad, power[0]), ("row", "col"))
        moved_probe = probe_now + summed_grad / (
            jnp.sum(summed_power) / (window * window) + tiny_value
        )
        power_new = jnp.sum(moved_probe * moved_probe)
        probe_now = moved_probe * jnp.sqrt(power_old / (power_new + tiny_value))
    return (current, probe_now)


def solution(mesh):
    rows, cols = mesh.shape["row"], mesh.shape["col"]

    def shards_here(*args):
        deep = Sums.chunk(rows, cols, args[1].shape[1])
        return (shards_by_kernel if deep and deep % 8 == 0 else shards)(*args)

    return jax.shard_map(
        shards_here,
        mesh=mesh,
        in_specs=(
            P(None, "row", "col"),
            P(),
            P("row", "col", None),
            P("row", "col", None, None),
            P("row", "col"),
        ),
        out_specs=(P(None, "row", "col"), P()),
        check_vma=False,
    )
```

```python
import functools
import math

import jax
import jax.numpy as jnp
import numpy as np
from jax import lax
from jax.experimental import pallas as pl
from jax.experimental.pallas import tpu as pltpu
from jax.sharding import PartitionSpec as P

MESH = pl.DeviceIdType.MESH
HALO = 128
OUTER = 2


smooth_floor = 0.5
object_step = 0.5
tiny_value = 1e-06


def shifted(value, axis, by):
    length = lax.axis_size(axis)
    pairs = [(i, i + by) for i in range(length) if 0 <= i + by < length]
    return lax.ppermute(value, axis, pairs)


def make_tables(length):
    half = length // 2
    first = np.arange(half)[:, None]
    second = np.arange(half)[None, :]
    tables = []
    for parity in range(2):
        angles = (first * (2 * second + parity) % length) * (-2.0 * math.pi / length)
        real = np.cos(angles) / math.sqrt(length)
        imag = np.sin(angles) / math.sqrt(length)
        tables.append(np.block([[real, imag], [-imag, real]]))
    tables += [tables[0].T, tables[1].T]
    stacked = np.stack(tables).astype(np.float32)
    upper = stacked.astype(jnp.bfloat16)
    lower = (stacked - upper.astype(np.float32)).astype(jnp.bfloat16)
    sorting = np.zeros((length, length), np.float32)
    sorting[np.arange(length), np.arange(length) // 2 + half * (np.arange(length) % 2)] = 1.0
    return np.concatenate([upper, lower, sorting.astype(jnp.bfloat16)[None]])


def split(value):
    upper = value.astype(jnp.bfloat16)
    lower = (value - upper.astype(jnp.float32)).astype(jnp.bfloat16)
    return upper, lower


def dot(left, right):
    return jnp.dot(left, right, preferred_element_type=jnp.float32)


def times_table(value, tables, index):
    upper, lower = split(value)
    return (
        dot(upper, tables[index]) + dot(lower, tables[index]) + dot(upper, tables[index + 4])
    )


def table_times(tables, index, value):
    upper, lower = split(value)
    return (
        dot(tables[index], upper) + dot(tables[index], lower) + dot(tables[index + 4], upper)
    )


def lanes(*parts):
    return jnp.concatenate(parts, axis=1)


def stack(*parts):
    return jnp.concatenate(parts, axis=0)


def halves_of_lanes(value):
    half = value.shape[1] // 2
    return value[:, :half], value[:, half:]


def halves_of_rows(value):
    half = value.shape[0] // 2
    return value[:half], value[half:]


def forward(real, imag, tables):
    real_l, real_r = halves_of_lanes(real)
    imag_l, imag_r = halves_of_lanes(imag)
    even = times_table(lanes(real_l + real_r, imag_l + imag_r), tables, 0)
    odd = times_table(lanes(real_l - real_r, imag_l - imag_r), tables, 1)
    even_t, even_b = halves_of_rows(even)
    odd_t, odd_b = halves_of_rows(odd)
    even_re, even_im = halves_of_lanes(even_t + even_b)
    odd_re, odd_im = halves_of_lanes(odd_t + odd_b)
    top = table_times(tables, 2, stack(lanes(even_re, odd_re), lanes(even_im, odd_im)))
    even_re, even_im = halves_of_lanes(even_t - even_b)
    odd_re, odd_im = halves_of_lanes(odd_t - odd_b)
    bottom = table_times(tables, 3, stack(lanes(even_re, odd_re), lanes(even_im, odd_im)))
    return top, bottom


def inverse(top, bottom, tables):
    top = table_times(tables, 0, top)
    bottom = table_times(tables, 1, bottom)
    upper_re, upper_im = halves_of_rows(top + bottom)
    lower_re, lower_im = halves_of_rows(top - bottom)
    even_ur, odd_ur = halves_of_lanes(upper_re)
    even_ui, odd_ui = halves_of_lanes(upper_im)
    even_lr, odd_lr = halves_of_lanes(lower_re)
    even_li, odd_li = halves_of_lanes(lower_im)
    even = times_table(stack(lanes(even_ur, even_ui), lanes(even_lr, even_li)), tables, 2)
    odd = times_table(stack(lanes(odd_ur, odd_ui), lanes(odd_lr, odd_li)), tables, 3)
    left_re, left_im = halves_of_lanes(even + odd)
    right_re, right_im = halves_of_lanes(even - odd)
    return lanes(left_re, right_re), lanes(left_im, right_im)


def sort_amplitudes(amp_ref, tables, hold, ordered):
    half = hold.shape[2] // 2
    for slot in range(amp_ref.shape[0]):
        upper, lower = split(amp_ref[slot])
        value = dot(upper, tables[8]) + dot(lower, tables[8])
        for side, part in enumerate(halves_of_lanes(value)):
            hold[slot, side] = part
            for parity in range(2):
                ordered[slot, parity, :, side * half : (side + 1) * half] = hold[
                    slot, side, pl.ds(parity, half, stride=2), :
                ]


def cut_window(slabs, part, first_row, first_col, window, margin):
    lane = lax.broadcasted_iota(jnp.int32, (window, margin), 1)
    inside = lane < margin - first_col
    turn = lax.rem(margin - first_col, margin)
    turned = [
        pltpu.roll(slabs[part, slab, pl.ds(first_row, window), :], turn, 1)
        for slab in range(slabs.shape[1])
    ]
    return lanes(*[jnp.where(inside, a, b) for a, b in zip(turned[:-1], turned[1:])])


def place_lanes(term, first_col, margin):
    window = term.shape[0]
    lane = lax.broadcasted_iota(jnp.int32, (window, margin), 1)
    inside = lane >= first_col
    turn = lax.rem(first_col, margin)
    turned = [
        pltpu.roll(term[:, at : at + margin], turn, 1) for at in range(0, term.shape[1], margin)
    ]
    empty = jnp.zeros((window, margin), term.dtype)
    return [jnp.where(inside, a, b) for a, b in zip(turned + [empty], [empty] + turned)]


def pass_over_windows(
    off_ref, cnt_ref, ext_ref, probe_ref, ordered, tables, grad_ref, pgrad_ref, slabs, padded, summed
):
    slot_count = ordered.shape[0]
    window = probe_ref.shape[1]
    ext_rows = ext_ref.shape[1]
    margin = ext_rows - window
    for part in range(2):
        for slab in range(slabs.shape[1]):
            slabs[part, slab] = ext_ref[part, :, slab * margin : (slab + 1) * margin]
    probe_re = probe_ref[0]
    probe_im = probe_ref[1]
    power = None
    for slot in range(slot_count):
        first_row = off_ref[0, 0, slot, 0]
        first_col = off_ref[0, 0, slot, 1]
        live = (slot < cnt_ref[0, 0]).astype(jnp.float32)
        win_re = cut_window(slabs, 0, first_row, first_col, window, margin)
        win_im = cut_window(slabs, 1, first_row, first_col, window, margin)
        spectrum = forward(
            probe_re * win_re - probe_im * win_im, probe_re * win_im + probe_im * win_re, tables
        )
        replaced = []
        for parity, hat in enumerate(spectrum):
            measured = ordered[slot, parity]
            hat_re, hat_im = halves_of_rows(hat)
            ratio = measured * lax.rsqrt(hat_re * hat_re + hat_im * hat_im + smooth_floor) - 1.0
            ratio = ratio * live
            replaced.append(stack(hat_re * ratio, hat_im * ratio))
        diff_re, diff_im = inverse(*replaced, tables)
        probe_terms = (win_re * diff_re + win_im * diff_im, win_re * diff_im - win_im * diff_re)
        for part, term in enumerate(probe_terms):
            pgrad_ref[part] = term if slot == 0 else pgrad_ref[part] + term
        squares = jnp.sum(win_re * win_re + win_im * win_im, axis=0, keepdims=True) * live
        power = squares if power is None else power + squares
        if slot == slot_count - 1:
            summed(power)
        terms = (probe_re * diff_re + probe_im * diff_im, probe_re * diff_im - probe_im * diff_re)
        for part, term in enumerate(terms):
            empty = jnp.zeros((margin, margin), jnp.float32)
            for slab, placed in enumerate(place_lanes(term, first_col, margin)):
                box = padded.at[slot, part, slab]
                box[:margin] = empty
                box[margin : margin + window] = placed
                box[margin + window :] = empty
                shown = box[pl.ds(margin - first_row, ext_rows), :]
                here = slice(slab * margin, (slab + 1) * margin)
                if slot == 0:
                    grad_ref[part, :, here] = shown
                else:
                    grad_ref[part, :, here] += shown


def pass_kernel(
    off_ref, cnt_ref, ext_ref, probe_ref, amp_ref, tables, grad_ref, pgrad_ref, power_ref, *scratch
):
    hold, ordered, slabs, padded = scratch
    sort_amplitudes(amp_ref, tables, hold, ordered)

    def summed(power):
        power_ref[...] = jnp.broadcast_to(power, power_ref.shape)

    pass_over_windows(
        off_ref, cnt_ref, ext_ref, probe_ref, ordered, tables, grad_ref, pgrad_ref, slabs, padded, summed
    )


def pass_scratch(slots, window, ext_rows, ext_cols):
    margin = ext_rows - window
    return [
        pltpu.VMEM((slots, 2, window, window // 2), jnp.float32),
        pltpu.VMEM((slots, 2, window // 2, window), jnp.float32),
        pltpu.VMEM((2, ext_cols // margin, ext_rows, margin), jnp.float32),
        pltpu.VMEM((slots, 2, ext_cols // margin, window + 2 * margin, margin), jnp.float32),
    ]


def one_pass(extended, probe, amplitudes, offsets, counts, tables):
    slots, window = amplitudes.shape[0], probe.shape[1]
    ext_rows, ext_cols = extended.shape[1:]
    smem = pl.BlockSpec(memory_space=pltpu.SMEM)
    vmem = pl.BlockSpec(memory_space=pltpu.VMEM)
    return pl.pallas_call(
        pass_kernel,
        out_shape=(
            jax.ShapeDtypeStruct(extended.shape, jnp.float32),
            jax.ShapeDtypeStruct(probe.shape, jnp.float32),
            jax.ShapeDtypeStruct((8, window), jnp.float32),
        ),
        in_specs=[smem, smem, vmem, vmem, vmem, vmem],
        out_specs=(vmem, vmem, vmem),
        scratch_shapes=pass_scratch(slots, window, ext_rows, ext_cols),
        compiler_params=pltpu.CompilerParams(vmem_limit_bytes=40 * 2**20),
        name="window_pass",
    )(offsets, counts, extended, probe, amplitudes, tables)


def remote(src, dst, send_sem, recv_sem, **where):
    return pltpu.make_async_remote_copy(
        src_ref=src,
        dst_ref=dst,
        send_sem=send_sem,
        recv_sem=recv_sem,
        device_id=where,
        device_id_type=MESH,
    )


class Place:
    def __init__(self):
        self.rows = lax.axis_size("row")
        self.cols = lax.axis_size("col")
        self.row = lax.axis_index("row")
        self.col = lax.axis_index("col")
        self.has_up = self.row > 0
        self.has_down = self.row < self.rows - 1
        self.has_left = self.col > 0
        self.has_right = self.col < self.cols - 1
        self.up = lax.max(self.row - 1, 0)
        self.down = lax.min(self.row + 1, self.rows - 1)
        self.left = lax.max(self.col - 1, 0)
        self.right = lax.min(self.col + 1, self.cols - 1)

    def other_row(self, step):
        return lax.rem(self.row + step, self.rows)

    def other_col(self, step):
        return lax.rem(self.col + step, self.cols)

    def greet(self):
        barrier = pltpu.get_barrier_semaphore()
        for step in range(1, self.cols):
            pl.semaphore_signal(
                barrier, inc=1, device_id={"col": self.other_col(step)}, device_id_type=MESH
            )
        for step in range(1, self.rows):
            pl.semaphore_signal(
                barrier, inc=1, device_id={"row": self.other_row(step)}, device_id_type=MESH
            )

    def await_greetings(self):
        pl.semaphore_wait(pltpu.get_barrier_semaphore(), self.rows + self.cols - 2)


class Halo:
    @staticmethod
    def scratch(tile_rows, tile_cols, margin):
        return [
            pltpu.VMEM((2, margin, tile_cols), jnp.float32),
            pltpu.VMEM((2, tile_rows, margin), jnp.float32),
            pltpu.VMEM((2, margin, margin), jnp.float32),
            pltpu.SemaphoreType.DMA((4,)),
            pltpu.SemaphoreType.DMA((4,)),
        ]

    def __init__(self, place, object_ref, below, beside, corner, sent, came):
        self.place, self.object_ref = place, object_ref
        self.below, self.beside, self.corner = below, beside, corner
        margin = corner.shape[1]
        self.margin = margin
        first, rest = pl.ds(0, margin), pl.ds(margin, below.shape[2] - margin)
        self.from_below = [
            remote(
                object_ref.at[:, first, cols],
                below.at[:, :, cols],
                sent.at[at],
                came.at[at],
                row=place.up,
            )
            for at, cols in ((0, first), (3, rest))
        ]
        self.from_beside = remote(
            object_ref.at[:, :, pl.ds(0, margin)], beside, sent.at[1], came.at[1], col=place.left
        )
        self.from_corner = remote(
            below.at[:, :, pl.ds(0, margin)], corner, sent.at[2], came.at[2], col=place.left
        )

    def start(self):
        pl.when(self.place.has_left)(self.from_beside.start)

        @pl.when(self.place.has_up)
        def _():
            for copy in self.from_below:
                copy.start()

    def finish(self, ext_ref):
        place, margin = self.place, self.margin
        _, tile_rows, tile_cols = self.object_ref.shape
        ext_ref[:, :tile_rows, :tile_cols] = self.object_ref[...]

        @pl.when(place.has_down)
        def _():
            self.from_below[0].wait_recv()
            pl.when(place.has_left)(self.from_corner.start)
            self.from_below[1].wait_recv()
            ext_ref[:, tile_rows:, :tile_cols] = self.below[...]

        @pl.when(jnp.logical_not(place.has_down))
        def _():
            ext_ref[:, tile_rows:, :] = jnp.zeros((2, margin, tile_cols + margin), jnp.float32)

        @pl.when(place.has_right)
        def _():
            self.from_beside.wait_recv()
            ext_ref[:, :tile_rows, tile_cols:] = self.beside[...]

            @pl.when(place.has_down)
            def _():
                self.from_corner.wait_recv()
                ext_ref[:, tile_rows:, tile_cols:] = self.corner[...]

        @pl.when(jnp.logical_not(place.has_right))
        def _():
            ext_ref[:, :, tile_cols:] = jnp.zeros((2, tile_rows + margin, margin), jnp.float32)

    def settle(self):
        place = self.place

        @pl.when(place.has_up)
        def _():
            for copy in self.from_below:
                copy.wait_send()

        pl.when(place.has_left)(self.from_beside.wait_send)
        pl.when(jnp.logical_and(place.has_left, place.has_down))(self.from_corner.wait_send)


class Rims:
    @staticmethod
    def scratch(tile_rows, tile_cols, margin):
        tall, wide = tile_rows + margin, tile_cols + margin
        return [
            pltpu.VMEM((2, tall, wide), jnp.float32),
            pltpu.VMEM((2, tall, margin), jnp.float32),
            pltpu.VMEM((2, tall, margin), jnp.float32),
            pltpu.VMEM((2, margin, tile_cols), jnp.float32),
            pltpu.VMEM((2, margin, tile_cols), jnp.float32),
            pltpu.VMEM((2, margin, margin), jnp.float32),
            pltpu.VMEM((2, margin, margin), jnp.float32),
            pltpu.SemaphoreType.DMA((8,)),
            pltpu.SemaphoreType.DMA((8,)),
        ]

    def __init__(self, place, last, grad, total, left, right, above, below, over, under, sent, came):
        self.place, self.last, self.grad, self.total = place, last, grad, total
        self.left, self.right, self.above, self.below = left, right, above, below
        self.over, self.under = over, under
        margin = over.shape[1]
        tile_rows, tile_cols = grad.shape[1] - margin, grad.shape[2] - margin
        self.sizes = margin, tile_rows, tile_cols
        first = pl.ds(0, margin)
        self.to_right = remote(
            grad.at[:, :, pl.ds(tile_cols, margin)], left, sent.at[0], came.at[0], col=place.right
        )
        self.to_left = remote(grad.at[:, :, first], right, sent.at[1], came.at[1], col=place.left)
        rest = pl.ds(margin, tile_cols - margin)
        self.to_down = [
            remote(
                total.at[:, pl.ds(tile_rows, margin), cols],
                above.at[:, :, cols],
                sent.at[at],
                came.at[at],
                row=place.down,
            )
            for at, cols in ((2, first), (6, rest))
        ]
        self.to_up = [
            remote(
                total.at[:, first, cols],
                below.at[:, :, cols],
                sent.at[at],
                came.at[at],
                row=place.up,
            )
            for at, cols in ((3, first), (7, rest))
        ]
        self.pass_over = remote(
            above.at[:, :, first], over, sent.at[4], came.at[4], col=place.left
        )
        self.pass_under = remote(
            below.at[:, :, first], under, sent.at[5], came.at[5], col=place.left
        )

    def start(self):
        pl.when(self.place.has_right)(self.to_right.start)
        if not self.last:
            pl.when(self.place.has_left)(self.to_left.start)

    def start_rows(self):
        place, grad, total = self.place, self.grad, self.total
        margin, tile_rows, tile_cols = self.sizes
        total[...] = grad[...]

        @pl.when(place.has_left)
        def _():
            self.to_right.wait_recv()
            total[:, :, :margin] += self.left[...]

        if not self.last:

            @pl.when(place.has_right)
            def _():
                self.to_left.wait_recv()
                total[:, :, tile_cols:] += self.right[...]

        for half in range(2):
            pl.when(place.has_down)(self.to_down[half].start)
            if not self.last:
                pl.when(place.has_up)(self.to_up[half].start)

    def pass_on(self):
        place = self.place
        if self.last:
            return

        @pl.when(place.has_up)
        def _():
            self.to_down[0].wait_recv()
            pl.when(place.has_left)(self.pass_over.start)

        @pl.when(place.has_down)
        def _():
            self.to_up[0].wait_recv()
            pl.when(place.has_left)(self.pass_under.start)

    def update_inside(self, old_ref, new_ref, factor):
        total = self.total
        margin, tile_rows, tile_cols = self.sizes
        new_ref[:, margin:tile_rows, :tile_cols] = (
            old_ref[:, margin:tile_rows, :tile_cols] + factor * total[:, margin:tile_rows, :tile_cols]
        )

    def finish(self, old_ref, new_ref, factor):
        place, total = self.place, self.total
        margin, tile_rows, tile_cols = self.sizes

        @pl.when(place.has_up)
        def _():
            if self.last:
                self.to_down[0].wait_recv()
            self.to_down[1].wait_recv()
            new_ref[:, :margin, :tile_cols] = old_ref[:, :margin, :tile_cols] + factor * (
                total[:, :margin, :tile_cols] + self.above[...]
            )

        @pl.when(jnp.logical_not(place.has_up))
        def _():
            new_ref[:, :margin, :tile_cols] = (
                old_ref[:, :margin, :tile_cols] + factor * total[:, :margin, :tile_cols]
            )

        if self.last:
            return

        @pl.when(place.has_down)
        def _():
            self.to_up[1].wait_recv()
            new_ref[:, tile_rows:, :tile_cols] = old_ref[:, tile_rows:, :tile_cols] + factor * (
                total[:, tile_rows:, :tile_cols] + self.below[...]
            )

        @pl.when(jnp.logical_not(place.has_down))
        def _():
            new_ref[:, tile_rows:, :] = jnp.zeros((2, margin, tile_cols + margin), jnp.float32)

        @pl.when(place.has_right)
        def _():
            new_ref[:, margin:tile_rows, tile_cols:] = (
                old_ref[:, margin:tile_rows, tile_cols:]
                + factor * total[:, margin:tile_rows, tile_cols:]
            )

            @pl.when(place.has_up)
            def _():
                self.pass_over.wait_recv()
                new_ref[:, :margin, tile_cols:] = old_ref[:, :margin, tile_cols:] + factor * (
                    total[:, :margin, tile_cols:] + self.over[...]
                )

            @pl.when(jnp.logical_not(place.has_up))
            def _():
                new_ref[:, :margin, tile_cols:] = (
                    old_ref[:, :margin, tile_cols:] + factor * total[:, :margin, tile_cols:]
                )

            @pl.when(place.has_down)
            def _():
                self.pass_under.wait_recv()
                new_ref[:, tile_rows:, tile_cols:] = old_ref[:, tile_rows:, tile_cols:] + factor * (
                    total[:, tile_rows:, tile_cols:] + self.under[...]
                )

        @pl.when(jnp.logical_not(place.has_right))
        def _():
            new_ref[:, :, tile_cols:] = jnp.zeros((2, tile_rows + margin, margin), jnp.float32)

    def settle(self):
        place = self.place
        pl.when(place.has_right)(self.to_right.wait_send)
        for half in range(2):
            pl.when(place.has_down)(self.to_down[half].wait_send)
            if not self.last:
                pl.when(place.has_up)(self.to_up[half].wait_send)
        if not self.last:
            pl.when(place.has_left)(self.to_left.wait_send)
            pl.when(jnp.logical_and(place.has_left, place.has_up))(self.pass_over.wait_send)
            pl.when(jnp.logical_and(place.has_left, place.has_down))(self.pass_under.wait_send)


class Sums:
    extra = 1

    @staticmethod
    def chunk(rows, cols, window):
        return 2 * window * window // 128 // (rows * cols)

    @staticmethod
    def group(rows):
        return max(size for size in range(1, rows + 1) if rows % size == 0 and size * size <= rows)

    @classmethod
    def scratch(cls, rows, cols, window):
        deep = cls.chunk(rows, cols, window)
        full = deep + cls.extra
        near = cls.group(rows)
        far = rows // near
        more_cols, more_near, more_far = (max(size - 1, 1) for size in (cols, near, far))
        return [
            pltpu.VMEM((cols, near, far, full, 128), jnp.float32),
            pltpu.VMEM((more_cols, near, far, full, 128), jnp.float32),
            pltpu.VMEM((near, far, full, 128), jnp.float32),
            pltpu.VMEM((more_near, far, full, 128), jnp.float32),
            pltpu.VMEM((far, full, 128), jnp.float32),
            pltpu.VMEM((more_far, full, 128), jnp.float32),
            pltpu.VMEM((cols, near, far, deep, 128), jnp.float32),
            pltpu.SemaphoreType.DMA((2, more_cols)),
            pltpu.SemaphoreType.DMA((2, 2, more_near)),
            pltpu.SemaphoreType.DMA((2, 2, more_far)),
            pltpu.SemaphoreType.DMA((2, more_cols, near)),
        ]

    def __init__(
        self, place, whole, from_cols, part, from_near, less, from_far, gathered, sems, sems2, sems3, sems4
    ):
        self.place, self.whole, self.from_cols, self.part = place, whole, from_cols, part
        self.from_near, self.less, self.from_far, self.gathered = from_near, less, from_far, gathered
        _, self.near, self.far, self.deep, _ = gathered.shape
        near, far = self.near, self.far
        self.at_far, self.at_near = place.row // near, lax.rem(place.row, near)

        def other_near(step):
            return lax.rem(self.at_near + step, near)

        def other_far(step):
            return lax.rem(self.at_far + step, far)

        self.over_cols = [
            remote(
                whole.at[place.other_col(step)],
                from_cols.at[step - 1],
                sems.at[0, step - 1],
                sems.at[1, step - 1],
                col=place.other_col(step),
            )
            for step in range(1, place.cols)
        ]
        self.over_near = [
            remote(
                part.at[other_near(step)],
                from_near.at[step - 1],
                sems2.at[0, 0, step - 1],
                sems2.at[0, 1, step - 1],
                row=self.at_far * near + other_near(step),
            )
            for step in range(1, near)
        ]
        self.over_far = [
            remote(
                less.at[other_far(step)],
                from_far.at[step - 1],
                sems3.at[0, 0, step - 1],
                sems3.at[0, 1, step - 1],
                row=other_far(step) * near + self.at_near,
            )
            for step in range(1, far)
        ]
        mine = gathered.at[place.col, self.at_near, self.at_far]
        self.back_far = [
            remote(
                mine,
                mine,
                sems3.at[1, 0, step - 1],
                sems3.at[1, 1, step - 1],
                row=other_far(step) * near + self.at_near,
            )
            for step in range(1, far)
        ]
        block = gathered.at[place.col, self.at_near]
        self.back_near = [
            remote(
                block,
                block,
                sems2.at[1, 0, step - 1],
                sems2.at[1, 1, step - 1],
                row=self.at_far * near + other_near(step),
            )
            for step in range(1, near)
        ]
        self.back_cols = []
        for step in range(near):
            block = gathered.at[place.col, other_near(near - step)]
            self.back_cols.append(
                [
                    remote(
                        block,
                        block,
                        sems4.at[0, other - 1, step],
                        sems4.at[1, other - 1, step],
                        col=place.other_col(other),
                    )
                    for other in range(1, place.cols)
                ]
            )

    def slots(self, window):
        per = window // self.deep
        for number in range(self.place.cols * self.place.rows):
            slab, at = divmod(number, per)
            half, side = divmod(slab, window // 128)
            here = (
                half,
                slice(at * self.deep, (at + 1) * self.deep),
                slice(side * 128, (side + 1) * 128),
            )
            rest, far = divmod(number, self.far)
            yield here, (rest // self.near, rest % self.near, far)

    def fill(self, pgrad_ref, power):
        window = pgrad_ref.shape[1]
        folded = sum(power[:, at : at + 128] for at in range(0, window, 128))
        for here, (col, near, far) in self.slots(window):
            self.whole[col, near, far, : self.deep] = pgrad_ref[here]
            self.whole[col, near, far, self.deep :] = folded

    def start(self):
        for copy in self.over_cols:
            copy.start()

    def start_near(self):
        self.part[...] = self.whole[self.place.col]
        for step, copy in enumerate(self.over_cols):
            copy.wait_recv()
            self.part[...] += self.from_cols[step]
        for copy in self.over_near:
            copy.start()

    def start_far(self):
        total = self.part[self.at_near]
        for step, copy in enumerate(self.over_near):
            copy.wait_recv()
            total = total + self.from_near[step]
        self.less[...] = total
        for copy in self.over_far:
            copy.start()

    def start_back(self):
        total = self.less[self.at_far]
        for step, copy in enumerate(self.over_far):
            copy.wait_recv()
            total = total + self.from_far[step]
        self.gathered[self.place.col, self.at_near, self.at_far] = total[: self.deep]
        for copy in self.back_far:
            copy.start()
        return jnp.sum(total[self.deep :])

    def start_back_near(self):
        for copy in self.back_far:
            copy.wait_recv()
        for copy in self.back_near + self.back_cols[0]:
            copy.start()

    def pass_on(self):
        for step, copy in enumerate(self.back_near):
            copy.wait_recv()
            for other in self.back_cols[step + 1]:
                other.start()

    def finish(self, power, probe_ref, new_ref):
        window = probe_ref.shape[1]
        for copies in self.back_cols:
            for copy in copies:
                copy.wait_recv()
        old = jnp.sum(probe_ref[...] * probe_ref[...], keepdims=True)
        scale = 1.0 / (power / (window * window) + tiny_value)
        for here, (col, near, far) in self.slots(window):
            new_ref[here] = probe_ref[here] + self.gathered[col, near, far] * scale
        moved = new_ref[...]
        new = jnp.sum(moved * moved, keepdims=True)
        new_ref[...] = moved * jnp.sqrt(old / (new + tiny_value))

    def settle(self):
        copies = self.over_cols + self.over_near + self.over_far + self.back_far + self.back_near
        for copy in copies + sum(self.back_cols, []):
            copy.wait_send()


def whole_kernel(
    counts_of, off_ref, cnt_ref, object_hbm, probe_hbm, amp_hbm, tab_hbm, out_ref, new_ref, *scratch
):
    scratch = list(scratch)
    groups = []
    for count in counts_of:
        groups.append(scratch[:count])
        del scratch[:count]
    own, pass_refs, halo_refs, *step_refs = groups
    object_ref, probe_ref, amp_ref, tab_ref, loads, ext_a, ext_b, probe_b, grad_ref, pgrad_ref = own
    hold, ordered, slabs, padded = pass_refs
    place = Place()
    place.greet()
    pairs = (
        (object_hbm, object_ref),
        (tab_hbm, tab_ref),
        (amp_hbm, amp_ref),
        (probe_hbm, probe_ref),
    )
    copies = [pltpu.make_async_copy(*pair, loads.at[at]) for at, pair in enumerate(pairs)]
    for copy in copies:
        copy.start()
    halo = Halo(place, object_ref, *halo_refs)
    place.await_greetings()
    copies[0].wait()
    halo.start()
    for copy in copies[1:]:
        copy.wait()
    sort_amplitudes(amp_ref, tab_ref, hold, ordered)
    halo.finish(ext_a)
    exts, probes = [ext_a, ext_b], [probe_ref, probe_b]
    for step in range(OUTER):
        last = step == OUTER - 1
        ext, probe = exts[step % 2], probes[step % 2]
        rim_refs, sum_refs = step_refs[2 * step : 2 * step + 2]
        rims = Rims(place, last, grad_ref, *rim_refs)
        sums = Sums(place, *sum_refs)

        def summed(power):
            sums.fill(pgrad_ref, power)
            sums.start()

        pass_over_windows(
            off_ref, cnt_ref, ext, probe, ordered, tab_ref, grad_ref, pgrad_ref, slabs, padded, summed
        )
        if last:
            exchange(rims, sums, ext, probe, out_ref, new_ref)
        else:
            exchange(rims, sums, ext, probe, exts[1 - step % 2], probes[1 - step % 2])
    halo.settle()


def exchange(rims, sums, ext_ref, probe_ref, out_ref, new_ref):
    window = probe_ref.shape[1]
    rims.start()
    sums.start_near()
    if not rims.last:
        rims.start_rows()
    sums.start_far()
    if rims.last:
        rims.start_rows()
    mean = jnp.sum(probe_ref[...] * probe_ref[...]) / (window * window)
    factor = object_step / (mean + tiny_value)
    power = sums.start_back()
    rims.update_inside(ext_ref, out_ref, factor)
    sums.start_back_near()
    rims.pass_on()
    sums.pass_on()
    rims.finish(ext_ref, out_ref, factor)
    sums.finish(power, probe_ref, new_ref)
    rims.settle()
    sums.settle()


def shards_by_kernel(object_field, probe_field, amplitudes, offsets, counts):
    tables = jnp.asarray(make_tables(probe_field.shape[1]))
    _, tile_rows, tile_cols = object_field.shape
    slots, window = amplitudes.shape[0], probe_field.shape[1]
    rows, cols = lax.axis_size("row"), lax.axis_size("col")
    extended = (2, tile_rows + HALO, tile_cols + HALO)
    own = [
        pltpu.VMEM(object_field.shape, jnp.float32),
        pltpu.VMEM(probe_field.shape, jnp.float32),
        pltpu.VMEM(amplitudes.shape, jnp.float32),
        pltpu.VMEM(tables.shape, jnp.bfloat16),
        pltpu.SemaphoreType.DMA((4,)),
        pltpu.VMEM(extended, jnp.float32),
        pltpu.VMEM(extended, jnp.float32),
        pltpu.VMEM(probe_field.shape, jnp.float32),
        pltpu.VMEM(extended, jnp.float32),
        pltpu.VMEM(probe_field.shape, jnp.float32),
    ]
    groups = [own, pass_scratch(slots, window, *extended[1:]), Halo.scratch(tile_rows, tile_cols, HALO)]
    for step in range(OUTER):
        groups.append(Rims.scratch(tile_rows, tile_cols, HALO))
        groups.append(Sums.scratch(rows, cols, window))
    smem = pl.BlockSpec(memory_space=pltpu.SMEM)
    vmem = pl.BlockSpec(memory_space=pltpu.VMEM)
    anywhere = pl.BlockSpec(memory_space=pl.ANY)
    return pl.pallas_call(
        functools.partial(whole_kernel, [len(group) for group in groups]),
        out_shape=(
            jax.ShapeDtypeStruct(object_field.shape, jnp.float32),
            jax.ShapeDtypeStruct(probe_field.shape, jnp.float32),
        ),
        in_specs=[smem, smem, anywhere, anywhere, anywhere, anywhere],
        out_specs=(vmem, vmem),
        scratch_shapes=sum(groups, []),
        compiler_params=pltpu.CompilerParams(
            collective_id=0, has_side_effects=True, vmem_limit_bytes=60 * 2**20
        ),
        name="refinement",
    )(offsets, counts, object_field, probe_field, amplitudes, tables)


def shards(object_field, probe_field, amplitudes, offsets, counts):
    tile_rows = object_field.shape[1]
    tile_cols = object_field.shape[2]
    window = probe_field.shape[1]
    margin = HALO
    tables = jnp.asarray(make_tables(window))
    current = object_field
    probe_now = probe_field
    for outer_step in range(OUTER):
        probe_mean = jnp.sum(probe_now * probe_now) / (window * window)
        lower_rows = shifted(current[:, :margin, :], "row", -1)
        taller = jnp.concatenate([current, lower_rows], axis=1)
        right_cols = shifted(taller[:, :, :margin], "col", -1)
        extended = jnp.concatenate([taller, right_cols], axis=2)
        grad_ext, probe_grad, power = one_pass(
            extended, probe_now, amplitudes, offsets, counts, tables
        )
        rim_right = shifted(grad_ext[:, :, tile_cols:], "col", 1)
        narrowed = grad_ext[:, :, :tile_cols]
        narrowed = jnp.concatenate(
            [narrowed[:, :, :margin] + rim_right, narrowed[:, :, margin:]], axis=2
        )
        rim_lower = shifted(narrowed[:, tile_rows:, :], "row", 1)
        tile_grad = jnp.concatenate(
            [narrowed[:, :margin, :] + rim_lower, narrowed[:, margin:tile_rows, :]], axis=1
        )
        current = current + object_step * tile_grad / (probe_mean + tiny_value)
        power_old = jnp.sum(probe_now * probe_now)
        summed_grad, summed_power = lax.psum((probe_grad, power[0]), ("row", "col"))
        moved_probe = probe_now + summed_grad / (
            jnp.sum(summed_power) / (window * window) + tiny_value
        )
        power_new = jnp.sum(moved_probe * moved_probe)
        probe_now = moved_probe * jnp.sqrt(power_old / (power_new + tiny_value))
    return (current, probe_now)


def solution(mesh):
    rows, cols = mesh.shape["row"], mesh.shape["col"]

    def shards_here(*args):
        deep = Sums.chunk(rows, cols, args[1].shape[1])
        return (shards_by_kernel if deep and deep % 8 == 0 else shards)(*args)

    return jax.shard_map(
        shards_here,
        mesh=mesh,
        in_specs=(
            P(None, "row", "col"),
            P(),
            P("row", "col", None),
            P("row", "col", None, None),
            P("row", "col"),
        ),
        out_specs=(P(None, "row", "col"), P()),
        check_vma=False,
    )
```

```python
import functools
import math

import jax
import jax.numpy as jnp
import numpy as np
from jax import lax
from jax.experimental import pallas as pl
from jax.experimental.pallas import tpu as pltpu
from jax.sharding import PartitionSpec as P

MESH = pl.DeviceIdType.MESH
HALO = 128
OUTER = 2


smooth_floor = 0.5
object_step = 0.5
tiny_value = 1e-06


def shifted(value, axis, by):
    length = lax.axis_size(axis)
    pairs = [(i, i + by) for i in range(length) if 0 <= i + by < length]
    return lax.ppermute(value, axis, pairs)


def make_tables(length):
    half = length // 2
    first = np.arange(half)[:, None]
    second = np.arange(half)[None, :]
    tables = []
    for parity in range(2):
        angles = (first * (2 * second + parity) % length) * (-2.0 * math.pi / length)
        real = np.cos(angles) / math.sqrt(length)
        imag = np.sin(angles) / math.sqrt(length)
        tables.append(np.block([[real, imag], [-imag, real]]))
    tables += [tables[0].T, tables[1].T]
    stacked = np.stack(tables).astype(np.float32)
    upper = stacked.astype(jnp.bfloat16)
    lower = (stacked - upper.astype(np.float32)).astype(jnp.bfloat16)
    sorting = np.zeros((length, length), np.float32)
    sorting[np.arange(length), np.arange(length) // 2 + half * (np.arange(length) % 2)] = 1.0
    return np.concatenate([upper, lower, sorting.astype(jnp.bfloat16)[None]])


def split(value):
    upper = value.astype(jnp.bfloat16)
    lower = (value - upper.astype(jnp.float32)).astype(jnp.bfloat16)
    return upper, lower


def dot(left, right):
    return jnp.dot(left, right, preferred_element_type=jnp.float32)


def times_table(value, tables, index):
    upper, lower = split(value)
    return (
        dot(upper, tables[index]) + dot(lower, tables[index]) + dot(upper, tables[index + 4])
    )


def table_times(tables, index, value):
    upper, lower = split(value)
    return (
        dot(tables[index], upper) + dot(tables[index], lower) + dot(tables[index + 4], upper)
    )


def lanes(*parts):
    return jnp.concatenate(parts, axis=1)


def stack(*parts):
    return jnp.concatenate(parts, axis=0)


def halves_of_lanes(value):
    half = value.shape[1] // 2
    return value[:, :half], value[:, half:]


def halves_of_rows(value):
    half = value.shape[0] // 2
    return value[:half], value[half:]


def forward(real, imag, tables):
    real_l, real_r = halves_of_lanes(real)
    imag_l, imag_r = halves_of_lanes(imag)
    even = times_table(lanes(real_l + real_r, imag_l + imag_r), tables, 0)
    odd = times_table(lanes(real_l - real_r, imag_l - imag_r), tables, 1)
    even_t, even_b = halves_of_rows(even)
    odd_t, odd_b = halves_of_rows(odd)
    even_re, even_im = halves_of_lanes(even_t + even_b)
    odd_re, odd_im = halves_of_lanes(odd_t + odd_b)
    top = table_times(tables, 2, stack(lanes(even_re, odd_re), lanes(even_im, odd_im)))
    even_re, even_im = halves_of_lanes(even_t - even_b)
    odd_re, odd_im = halves_of_lanes(odd_t - odd_b)
    bottom = table_times(tables, 3, stack(lanes(even_re, odd_re), lanes(even_im, odd_im)))
    return top, bottom


def inverse(top, bottom, tables):
    top = table_times(tables, 0, top)
    bottom = table_times(tables, 1, bottom)
    upper_re, upper_im = halves_of_rows(top + bottom)
    lower_re, lower_im = halves_of_rows(top - bottom)
    even_ur, odd_ur = halves_of_lanes(upper_re)
    even_ui, odd_ui = halves_of_lanes(upper_im)
    even_lr, odd_lr = halves_of_lanes(lower_re)
    even_li, odd_li = halves_of_lanes(lower_im)
    even = times_table(stack(lanes(even_ur, even_ui), lanes(even_lr, even_li)), tables, 2)
    odd = times_table(stack(lanes(odd_ur, odd_ui), lanes(odd_lr, odd_li)), tables, 3)
    left_re, left_im = halves_of_lanes(even + odd)
    right_re, right_im = halves_of_lanes(even - odd)
    return lanes(left_re, right_re), lanes(left_im, right_im)


def sort_amplitudes(amp_ref, tables, hold, ordered):
    half = hold.shape[2] // 2
    for slot in range(amp_ref.shape[0]):
        upper, lower = split(amp_ref[slot])
        value = dot(upper, tables[8]) + dot(lower, tables[8])
        for side, part in enumerate(halves_of_lanes(value)):
            hold[slot, side] = part
            for parity in range(2):
                ordered[slot, parity, :, side * half : (side + 1) * half] = hold[
                    slot, side, pl.ds(parity, half, stride=2), :
                ]


def cut_window(slabs, part, first_row, first_col, window, margin):
    lane = lax.broadcasted_iota(jnp.int32, (window, margin), 1)
    inside = lane < margin - first_col
    turn = lax.rem(margin - first_col, margin)
    turned = [
        pltpu.roll(slabs[part, slab, pl.ds(first_row, window), :], turn, 1)
        for slab in range(slabs.shape[1])
    ]
    return lanes(*[jnp.where(inside, a, b) for a, b in zip(turned[:-1], turned[1:])])


def place_lanes(term, first_col, margin):
    window = term.shape[0]
    lane = lax.broadcasted_iota(jnp.int32, (window, margin), 1)
    inside = lane >= first_col
    turn = lax.rem(first_col, margin)
    turned = [
        pltpu.roll(term[:, at : at + margin], turn, 1) for at in range(0, term.shape[1], margin)
    ]
    empty = jnp.zeros((window, margin), term.dtype)
    return [jnp.where(inside, a, b) for a, b in zip(turned + [empty], [empty] + turned)]


def pass_over_windows(
    off_ref, cnt_ref, ext_ref, probe_ref, ordered, tables, grad_ref, pgrad_ref, slabs, padded, summed
):
    slot_count = ordered.shape[0]
    window = probe_ref.shape[1]
    ext_rows = ext_ref.shape[1]
    margin = ext_rows - window
    for part in range(2):
        for slab in range(slabs.shape[1]):
            slabs[part, slab] = ext_ref[part, :, slab * margin : (slab + 1) * margin]
    probe_re = probe_ref[0]
    probe_im = probe_ref[1]
    power = None
    for slot in range(slot_count):
        first_row = off_ref[0, 0, slot, 0]
        first_col = off_ref[0, 0, slot, 1]
        live = (slot < cnt_ref[0, 0]).astype(jnp.float32)
        win_re = cut_window(slabs, 0, first_row, first_col, window, margin)
        win_im = cut_window(slabs, 1, first_row, first_col, window, margin)
        spectrum = forward(
            probe_re * win_re - probe_im * win_im, probe_re * win_im + probe_im * win_re, tables
        )
        replaced = []
        for parity, hat in enumerate(spectrum):
            measured = ordered[slot, parity]
            hat_re, hat_im = halves_of_rows(hat)
            ratio = measured * lax.rsqrt(hat_re * hat_re + hat_im * hat_im + smooth_floor) - 1.0
            ratio = ratio * live
            replaced.append(stack(hat_re * ratio, hat_im * ratio))
        diff_re, diff_im = inverse(*replaced, tables)
        probe_terms = (win_re * diff_re + win_im * diff_im, win_re * diff_im - win_im * diff_re)
        for part, term in enumerate(probe_terms):
            pgrad_ref[part] = term if slot == 0 else pgrad_ref[part] + term
        squares = jnp.sum(win_re * win_re + win_im * win_im, axis=0, keepdims=True) * live
        power = squares if power is None else power + squares
        if slot == slot_count - 1:
            summed(power)
        terms = (probe_re * diff_re + probe_im * diff_im, probe_re * diff_im - probe_im * diff_re)
        for part, term in enumerate(terms):
            empty = jnp.zeros((margin, margin), jnp.float32)
            for slab, placed in enumerate(place_lanes(term, first_col, margin)):
                box = padded.at[slot, part, slab]
                box[:margin] = empty
                box[margin : margin + window] = placed
                box[margin + window :] = empty
                shown = box[pl.ds(margin - first_row, ext_rows), :]
                here = slice(slab * margin, (slab + 1) * margin)
                if slot == 0:
                    grad_ref[part, :, here] = shown
                else:
                    grad_ref[part, :, here] += shown


def pass_kernel(
    off_ref, cnt_ref, ext_ref, probe_ref, amp_ref, tables, grad_ref, pgrad_ref, power_ref, *scratch
):
    hold, ordered, slabs, padded = scratch
    sort_amplitudes(amp_ref, tables, hold, ordered)

    def summed(power):
        power_ref[...] = jnp.broadcast_to(power, power_ref.shape)

    pass_over_windows(
        off_ref, cnt_ref, ext_ref, probe_ref, ordered, tables, grad_ref, pgrad_ref, slabs, padded, summed
    )


def pass_scratch(slots, window, ext_rows, ext_cols):
    margin = ext_rows - window
    return [
        pltpu.VMEM((slots, 2, window, window // 2), jnp.float32),
        pltpu.VMEM((slots, 2, window // 2, window), jnp.float32),
        pltpu.VMEM((2, ext_cols // margin, ext_rows, margin), jnp.float32),
        pltpu.VMEM((slots, 2, ext_cols // margin, window + 2 * margin, margin), jnp.float32),
    ]


def one_pass(extended, probe, amplitudes, offsets, counts, tables):
    slots, window = amplitudes.shape[0], probe.shape[1]
    ext_rows, ext_cols = extended.shape[1:]
    smem = pl.BlockSpec(memory_space=pltpu.SMEM)
    vmem = pl.BlockSpec(memory_space=pltpu.VMEM)
    return pl.pallas_call(
        pass_kernel,
        out_shape=(
            jax.ShapeDtypeStruct(extended.shape, jnp.float32),
            jax.ShapeDtypeStruct(probe.shape, jnp.float32),
            jax.ShapeDtypeStruct((8, window), jnp.float32),
        ),
        in_specs=[smem, smem, vmem, vmem, vmem, vmem],
        out_specs=(vmem, vmem, vmem),
        scratch_shapes=pass_scratch(slots, window, ext_rows, ext_cols),
        compiler_params=pltpu.CompilerParams(vmem_limit_bytes=40 * 2**20),
        name="window_pass",
    )(offsets, counts, extended, probe, amplitudes, tables)


def remote(src, dst, send_sem, recv_sem, **where):
    return pltpu.make_async_remote_copy(
        src_ref=src,
        dst_ref=dst,
        send_sem=send_sem,
        recv_sem=recv_sem,
        device_id=where,
        device_id_type=MESH,
    )


class Place:
    def __init__(self):
        self.rows = lax.axis_size("row")
        self.cols = lax.axis_size("col")
        self.row = lax.axis_index("row")
        self.col = lax.axis_index("col")
        self.has_up = self.row > 0
        self.has_down = self.row < self.rows - 1
        self.has_left = self.col > 0
        self.has_right = self.col < self.cols - 1
        self.up = lax.max(self.row - 1, 0)
        self.down = lax.min(self.row + 1, self.rows - 1)
        self.left = lax.max(self.col - 1, 0)
        self.right = lax.min(self.col + 1, self.cols - 1)

    def other_row(self, step):
        return lax.rem(self.row + step, self.rows)

    def other_col(self, step):
        return lax.rem(self.col + step, self.cols)

    def greet(self):
        barrier = pltpu.get_barrier_semaphore()
        for step in range(1, self.cols):
            pl.semaphore_signal(
                barrier, inc=1, device_id={"col": self.other_col(step)}, device_id_type=MESH
            )
        for step in range(1, self.rows):
            pl.semaphore_signal(
                barrier, inc=1, device_id={"row": self.other_row(step)}, device_id_type=MESH
            )

    def await_greetings(self):
        pl.semaphore_wait(pltpu.get_barrier_semaphore(), self.rows + self.cols - 2)


class Halo:
    @staticmethod
    def scratch(tile_rows, tile_cols, margin):
        return [
            pltpu.VMEM((2, margin, tile_cols), jnp.float32),
            pltpu.VMEM((2, tile_rows, margin), jnp.float32),
            pltpu.VMEM((2, margin, margin), jnp.float32),
            pltpu.SemaphoreType.DMA((4,)),
            pltpu.SemaphoreType.DMA((4,)),
        ]

    def __init__(self, place, object_ref, below, beside, corner, sent, came):
        self.place, self.object_ref = place, object_ref
        self.below, self.beside, self.corner = below, beside, corner
        margin = corner.shape[1]
        self.margin = margin
        first, rest = pl.ds(0, margin), pl.ds(margin, below.shape[2] - margin)
        self.from_below = [
            remote(
                object_ref.at[:, first, cols],
                below.at[:, :, cols],
                sent.at[at],
                came.at[at],
                row=place.up,
            )
            for at, cols in ((0, first), (3, rest))
        ]
        self.from_beside = remote(
            object_ref.at[:, :, pl.ds(0, margin)], beside, sent.at[1], came.at[1], col=place.left
        )
        self.from_corner = remote(
            below.at[:, :, pl.ds(0, margin)], corner, sent.at[2], came.at[2], col=place.left
        )

    def start(self):
        pl.when(self.place.has_left)(self.from_beside.start)

        @pl.when(self.place.has_up)
        def _():
            for copy in self.from_below:
                copy.start()

    def finish(self, ext_ref):
        place, margin = self.place, self.margin
        _, tile_rows, tile_cols = self.object_ref.shape
        ext_ref[:, :tile_rows, :tile_cols] = self.object_ref[...]

        @pl.when(place.has_down)
        def _():
            self.from_below[0].wait_recv()
            pl.when(place.has_left)(self.from_corner.start)
            self.from_below[1].wait_recv()
            ext_ref[:, tile_rows:, :tile_cols] = self.below[...]

        @pl.when(jnp.logical_not(place.has_down))
        def _():
            ext_ref[:, tile_rows:, :] = jnp.zeros((2, margin, tile_cols + margin), jnp.float32)

        @pl.when(place.has_right)
        def _():
            self.from_beside.wait_recv()
            ext_ref[:, :tile_rows, tile_cols:] = self.beside[...]

            @pl.when(place.has_down)
            def _():
                self.from_corner.wait_recv()
                ext_ref[:, tile_rows:, tile_cols:] = self.corner[...]

        @pl.when(jnp.logical_not(place.has_right))
        def _():
            ext_ref[:, :, tile_cols:] = jnp.zeros((2, tile_rows + margin, margin), jnp.float32)

    def settle(self):
        place = self.place

        @pl.when(place.has_up)
        def _():
            for copy in self.from_below:
                copy.wait_send()

        pl.when(place.has_left)(self.from_beside.wait_send)
        pl.when(jnp.logical_and(place.has_left, place.has_down))(self.from_corner.wait_send)


class Rims:
    @staticmethod
    def scratch(tile_rows, tile_cols, margin):
        tall, wide = tile_rows + margin, tile_cols + margin
        return [
            pltpu.VMEM((2, tall, wide), jnp.float32),
            pltpu.VMEM((2, tall, margin), jnp.float32),
            pltpu.VMEM((2, tall, margin), jnp.float32),
            pltpu.VMEM((2, margin, tile_cols), jnp.float32),
            pltpu.VMEM((2, margin, tile_cols), jnp.float32),
            pltpu.VMEM((2, margin, margin), jnp.float32),
            pltpu.VMEM((2, margin, margin), jnp.float32),
            pltpu.SemaphoreType.DMA((8,)),
            pltpu.SemaphoreType.DMA((8,)),
        ]

    def __init__(self, place, last, grad, total, left, right, above, below, over, under, sent, came):
        self.place, self.last, self.grad, self.total = place, last, grad, total
        self.left, self.right, self.above, self.below = left, right, above, below
        self.over, self.under = over, under
        margin = over.shape[1]
        tile_rows, tile_cols = grad.shape[1] - margin, grad.shape[2] - margin
        self.sizes = margin, tile_rows, tile_cols
        first = pl.ds(0, margin)
        self.to_right = remote(
            grad.at[:, :, pl.ds(tile_cols, margin)], left, sent.at[0], came.at[0], col=place.right
        )
        self.to_left = remote(grad.at[:, :, first], right, sent.at[1], came.at[1], col=place.left)
        rest = pl.ds(margin, tile_cols - margin)
        self.to_down = [
            remote(
                total.at[:, pl.ds(tile_rows, margin), cols],
                above.at[:, :, cols],
                sent.at[at],
                came.at[at],
                row=place.down,
            )
            for at, cols in ((2, first), (6, rest))
        ]
        self.to_up = [
            remote(
                total.at[:, first, cols],
                below.at[:, :, cols],
                sent.at[at],
                came.at[at],
                row=place.up,
            )
            for at, cols in ((3, first), (7, rest))
        ]
        self.pass_over = remote(
            above.at[:, :, first], over, sent.at[4], came.at[4], col=place.left
        )
        self.pass_under = remote(
            below.at[:, :, first], under, sent.at[5], came.at[5], col=place.left
        )

    def start(self):
        pl.when(self.place.has_right)(self.to_right.start)
        if not self.last:
            pl.when(self.place.has_left)(self.to_left.start)

    def start_rows(self):
        place, grad, total = self.place, self.grad, self.total
        margin, tile_rows, tile_cols = self.sizes
        total[...] = grad[...]

        @pl.when(place.has_left)
        def _():
            self.to_right.wait_recv()
            total[:, :, :margin] += self.left[...]

        if not self.last:

            @pl.when(place.has_right)
            def _():
                self.to_left.wait_recv()
                total[:, :, tile_cols:] += self.right[...]

        for half in range(2):
            pl.when(place.has_down)(self.to_down[half].start)
            if not self.last:
                pl.when(place.has_up)(self.to_up[half].start)

    def pass_on(self):
        place = self.place
        if self.last:
            return

        @pl.when(place.has_up)
        def _():
            self.to_down[0].wait_recv()
            pl.when(place.has_left)(self.pass_over.start)

        @pl.when(place.has_down)
        def _():
            self.to_up[0].wait_recv()
            pl.when(place.has_left)(self.pass_under.start)

    def update_inside(self, old_ref, new_ref, factor):
        total = self.total
        margin, tile_rows, tile_cols = self.sizes
        new_ref[:, margin:tile_rows, :tile_cols] = (
            old_ref[:, margin:tile_rows, :tile_cols] + factor * total[:, margin:tile_rows, :tile_cols]
        )

    def finish(self, old_ref, new_ref, factor):
        place, total = self.place, self.total
        margin, tile_rows, tile_cols = self.sizes

        @pl.when(place.has_up)
        def _():
            if self.last:
                self.to_down[0].wait_recv()
            self.to_down[1].wait_recv()
            new_ref[:, :margin, :tile_cols] = old_ref[:, :margin, :tile_cols] + factor * (
                total[:, :margin, :tile_cols] + self.above[...]
            )

        @pl.when(jnp.logical_not(place.has_up))
        def _():
            new_ref[:, :margin, :tile_cols] = (
                old_ref[:, :margin, :tile_cols] + factor * total[:, :margin, :tile_cols]
            )

        if self.last:
            return

        @pl.when(place.has_down)
        def _():
            self.to_up[1].wait_recv()
            new_ref[:, tile_rows:, :tile_cols] = old_ref[:, tile_rows:, :tile_cols] + factor * (
                total[:, tile_rows:, :tile_cols] + self.below[...]
            )

        @pl.when(jnp.logical_not(place.has_down))
        def _():
            new_ref[:, tile_rows:, :] = jnp.zeros((2, margin, tile_cols + margin), jnp.float32)

        @pl.when(place.has_right)
        def _():
            new_ref[:, margin:tile_rows, tile_cols:] = (
                old_ref[:, margin:tile_rows, tile_cols:]
                + factor * total[:, margin:tile_rows, tile_cols:]
            )

            @pl.when(place.has_up)
            def _():
                self.pass_over.wait_recv()
                new_ref[:, :margin, tile_cols:] = old_ref[:, :margin, tile_cols:] + factor * (
                    total[:, :margin, tile_cols:] + self.over[...]
                )

            @pl.when(jnp.logical_not(place.has_up))
            def _():
                new_ref[:, :margin, tile_cols:] = (
                    old_ref[:, :margin, tile_cols:] + factor * total[:, :margin, tile_cols:]
                )

            @pl.when(place.has_down)
            def _():
                self.pass_under.wait_recv()
                new_ref[:, tile_rows:, tile_cols:] = old_ref[:, tile_rows:, tile_cols:] + factor * (
                    total[:, tile_rows:, tile_cols:] + self.under[...]
                )

        @pl.when(jnp.logical_not(place.has_right))
        def _():
            new_ref[:, :, tile_cols:] = jnp.zeros((2, tile_rows + margin, margin), jnp.float32)

    def settle(self):
        place = self.place
        pl.when(place.has_right)(self.to_right.wait_send)
        for half in range(2):
            pl.when(place.has_down)(self.to_down[half].wait_send)
            if not self.last:
                pl.when(place.has_up)(self.to_up[half].wait_send)
        if not self.last:
            pl.when(place.has_left)(self.to_left.wait_send)
            pl.when(jnp.logical_and(place.has_left, place.has_up))(self.pass_over.wait_send)
            pl.when(jnp.logical_and(place.has_left, place.has_down))(self.pass_under.wait_send)


class Sums:
    extra = 1

    @staticmethod
    def chunk(rows, cols, window):
        return 2 * window * window // 128 // (rows * cols)

    @staticmethod
    def group(rows):
        return max(size for size in range(1, rows + 1) if rows % size == 0 and size * size <= rows)

    @classmethod
    def scratch(cls, rows, cols, window):
        deep = cls.chunk(rows, cols, window)
        full = deep + cls.extra
        near = cls.group(rows)
        far = rows // near
        more_cols, more_near, more_far = (max(size - 1, 1) for size in (cols, near, far))
        return [
            pltpu.VMEM((cols, near, far, full, 128), jnp.float32),
            pltpu.VMEM((more_cols, near, far, full, 128), jnp.float32),
            pltpu.VMEM((near, far, full, 128), jnp.float32),
            pltpu.VMEM((more_near, far, full, 128), jnp.float32),
            pltpu.VMEM((far, full, 128), jnp.float32),
            pltpu.VMEM((more_far, full, 128), jnp.float32),
            pltpu.VMEM((cols, near, far, deep, 128), jnp.float32),
            pltpu.SemaphoreType.DMA((2, more_cols, near)),
            pltpu.SemaphoreType.DMA((2, 2, more_near)),
            pltpu.SemaphoreType.DMA((2, 2, more_far)),
            pltpu.SemaphoreType.DMA((2, more_cols, near)),
        ]

    def __init__(
        self, place, whole, from_cols, part, from_near, less, from_far, gathered, sems, sems2, sems3, sems4
    ):
        self.place, self.whole, self.from_cols, self.part = place, whole, from_cols, part
        self.from_near, self.less, self.from_far, self.gathered = from_near, less, from_far, gathered
        _, self.near, self.far, self.deep, _ = gathered.shape
        near, far = self.near, self.far
        self.at_far, self.at_near = place.row // near, lax.rem(place.row, near)

        def other_near(step):
            return lax.rem(self.at_near + step, near)

        def other_far(step):
            return lax.rem(self.at_far + step, far)

        self.other_near = other_near
        self.over_cols = [
            [
                remote(
                    whole.at[place.other_col(step), other_near(block)],
                    from_cols.at[step - 1, other_near(block)],
                    sems.at[0, step - 1, block],
                    sems.at[1, step - 1, block],
                    col=place.other_col(step),
                )
                for step in range(1, place.cols)
            ]
            for block in [*range(1, near), 0]
        ]
        self.over_near = [
            remote(
                part.at[other_near(step)],
                from_near.at[step - 1],
                sems2.at[0, 0, step - 1],
                sems2.at[0, 1, step - 1],
                row=self.at_far * near + other_near(step),
            )
            for step in range(1, near)
        ]
        self.over_far = [
            remote(
                less.at[other_far(step)],
                from_far.at[step - 1],
                sems3.at[0, 0, step - 1],
                sems3.at[0, 1, step - 1],
                row=other_far(step) * near + self.at_near,
            )
            for step in range(1, far)
        ]
        mine = gathered.at[place.col, self.at_near, self.at_far]
        self.back_far = [
            remote(
                mine,
                mine,
                sems3.at[1, 0, step - 1],
                sems3.at[1, 1, step - 1],
                row=other_far(step) * near + self.at_near,
            )
            for step in range(1, far)
        ]
        block = gathered.at[place.col, self.at_near]
        self.back_near = [
            remote(
                block,
                block,
                sems2.at[1, 0, step - 1],
                sems2.at[1, 1, step - 1],
                row=self.at_far * near + other_near(step),
            )
            for step in range(1, near)
        ]
        self.back_cols = []
        for step in range(near):
            block = gathered.at[place.col, other_near(near - step)]
            self.back_cols.append(
                [
                    remote(
                        block,
                        block,
                        sems4.at[0, other - 1, step],
                        sems4.at[1, other - 1, step],
                        col=place.other_col(other),
                    )
                    for other in range(1, place.cols)
                ]
            )

    def slots(self, window):
        per = window // self.deep
        for number in range(self.place.cols * self.place.rows):
            slab, at = divmod(number, per)
            half, side = divmod(slab, window // 128)
            here = (
                half,
                slice(at * self.deep, (at + 1) * self.deep),
                slice(side * 128, (side + 1) * 128),
            )
            rest, far = divmod(number, self.far)
            yield here, (rest // self.near, rest % self.near, far)

    def fill(self, pgrad_ref, power):
        window = pgrad_ref.shape[1]
        folded = sum(power[:, at : at + 128] for at in range(0, window, 128))
        for here, (col, near, far) in self.slots(window):
            self.whole[col, near, far, : self.deep] = pgrad_ref[here]
            self.whole[col, near, far, self.deep :] = folded

    def start(self):
        for copies in self.over_cols:
            for copy in copies:
                copy.start()

    def start_near(self):
        for block, copies in zip([*range(1, self.near), 0], self.over_cols):
            at = self.other_near(block)
            total = self.whole[self.place.col, at]
            for step, copy in enumerate(copies):
                copy.wait_recv()
                total = total + self.from_cols[step, at]
            self.part[at] = total
            if block:
                self.over_near[block - 1].start()

    def start_far(self):
        total = self.part[self.at_near]
        for step, copy in enumerate(self.over_near):
            copy.wait_recv()
            total = total + self.from_near[step]
        self.less[...] = total
        for copy in self.over_far:
            copy.start()

    def start_back(self):
        total = self.less[self.at_far]
        for step, copy in enumerate(self.over_far):
            copy.wait_recv()
            total = total + self.from_far[step]
        self.gathered[self.place.col, self.at_near, self.at_far] = total[: self.deep]
        for copy in self.back_far:
            copy.start()
        return jnp.sum(total[self.deep :])

    def start_back_near(self):
        for copy in self.back_far:
            copy.wait_recv()
        for copy in self.back_near + self.back_cols[0]:
            copy.start()

    def pass_on(self):
        for step, copy in enumerate(self.back_near):
            copy.wait_recv()
            for other in self.back_cols[step + 1]:
                other.start()

    def finish(self, power, probe_ref, new_ref):
        window = probe_ref.shape[1]
        for copies in self.back_cols:
            for copy in copies:
                copy.wait_recv()
        old = jnp.sum(probe_ref[...] * probe_ref[...], keepdims=True)
        scale = 1.0 / (power / (window * window) + tiny_value)
        for here, (col, near, far) in self.slots(window):
            new_ref[here] = probe_ref[here] + self.gathered[col, near, far] * scale
        moved = new_ref[...]
        new = jnp.sum(moved * moved, keepdims=True)
        new_ref[...] = moved * jnp.sqrt(old / (new + tiny_value))

    def settle(self):
        copies = self.over_near + self.over_far + self.back_far + self.back_near
        for copy in copies + sum(self.over_cols + self.back_cols, []):
            copy.wait_send()


def whole_kernel(
    counts_of, off_ref, cnt_ref, object_hbm, probe_hbm, amp_hbm, tab_hbm, out_ref, new_ref, *scratch
):
    scratch = list(scratch)
    groups = []
    for count in counts_of:
        groups.append(scratch[:count])
        del scratch[:count]
    own, pass_refs, halo_refs, *step_refs = groups
    object_ref, probe_ref, amp_ref, tab_ref, loads, ext_a, ext_b, probe_b, grad_ref, pgrad_ref = own
    hold, ordered, slabs, padded = pass_refs
    place = Place()
    place.greet()
    pairs = (
        (object_hbm, object_ref),
        (tab_hbm, tab_ref),
        (amp_hbm, amp_ref),
        (probe_hbm, probe_ref),
    )
    copies = [pltpu.make_async_copy(*pair, loads.at[at]) for at, pair in enumerate(pairs)]
    for copy in copies:
        copy.start()
    halo = Halo(place, object_ref, *halo_refs)
    place.await_greetings()
    copies[0].wait()
    halo.start()
    for copy in copies[1:]:
        copy.wait()
    sort_amplitudes(amp_ref, tab_ref, hold, ordered)
    halo.finish(ext_a)
    exts, probes = [ext_a, ext_b], [probe_ref, probe_b]
    for step in range(OUTER):
        last = step == OUTER - 1
        ext, probe = exts[step % 2], probes[step % 2]
        rim_refs, sum_refs = step_refs[2 * step : 2 * step + 2]
        rims = Rims(place, last, grad_ref, *rim_refs)
        sums = Sums(place, *sum_refs)

        def summed(power):
            sums.fill(pgrad_ref, power)
            sums.start()

        pass_over_windows(
            off_ref, cnt_ref, ext, probe, ordered, tab_ref, grad_ref, pgrad_ref, slabs, padded, summed
        )
        if last:
            exchange(rims, sums, ext, probe, out_ref, new_ref)
        else:
            exchange(rims, sums, ext, probe, exts[1 - step % 2], probes[1 - step % 2])
    halo.settle()


def exchange(rims, sums, ext_ref, probe_ref, out_ref, new_ref):
    window = probe_ref.shape[1]
    rims.start()
    sums.start_near()
    if not rims.last:
        rims.start_rows()
    sums.start_far()
    if rims.last:
        rims.start_rows()
    mean = jnp.sum(probe_ref[...] * probe_ref[...]) / (window * window)
    factor = object_step / (mean + tiny_value)
    power = sums.start_back()
    rims.update_inside(ext_ref, out_ref, factor)
    sums.start_back_near()
    rims.pass_on()
    sums.pass_on()
    rims.finish(ext_ref, out_ref, factor)
    sums.finish(power, probe_ref, new_ref)
    rims.settle()
    sums.settle()


def hand_over_kernel(object_ref, probe_ref, object_out, probe_out, sems):
    copies = [
        pltpu.make_async_copy(object_ref, object_out, sems.at[0]),
        pltpu.make_async_copy(probe_ref, probe_out, sems.at[1]),
    ]
    for copy in copies:
        copy.start()
    for copy in copies:
        copy.wait()


def hand_over(*results):
    anywhere = pl.BlockSpec(memory_space=pl.ANY)
    return pl.pallas_call(
        hand_over_kernel,
        out_shape=tuple(jax.ShapeDtypeStruct(value.shape, value.dtype) for value in results),
        in_specs=[anywhere] * 2,
        out_specs=(anywhere, anywhere),
        scratch_shapes=[pltpu.SemaphoreType.DMA((2,))],
        compiler_params=pltpu.CompilerParams(vmem_limit_bytes=60 * 2**20),
        name="hand_over",
    )(*results)


def shards_by_kernel(object_field, probe_field, amplitudes, offsets, counts):
    tables = jnp.asarray(make_tables(probe_field.shape[1]))
    _, tile_rows, tile_cols = object_field.shape
    slots, window = amplitudes.shape[0], probe_field.shape[1]
    rows, cols = lax.axis_size("row"), lax.axis_size("col")
    extended = (2, tile_rows + HALO, tile_cols + HALO)
    own = [
        pltpu.VMEM(object_field.shape, jnp.float32),
        pltpu.VMEM(probe_field.shape, jnp.float32),
        pltpu.VMEM(amplitudes.shape, jnp.float32),
        pltpu.VMEM(tables.shape, jnp.bfloat16),
        pltpu.SemaphoreType.DMA((4,)),
        pltpu.VMEM(extended, jnp.float32),
        pltpu.VMEM(extended, jnp.float32),
        pltpu.VMEM(probe_field.shape, jnp.float32),
        pltpu.VMEM(extended, jnp.float32),
        pltpu.VMEM(probe_field.shape, jnp.float32),
    ]
    groups = [own, pass_scratch(slots, window, *extended[1:]), Halo.scratch(tile_rows, tile_cols, HALO)]
    for step in range(OUTER):
        groups.append(Rims.scratch(tile_rows, tile_cols, HALO))
        groups.append(Sums.scratch(rows, cols, window))
    smem = pl.BlockSpec(memory_space=pltpu.SMEM)
    vmem = pl.BlockSpec(memory_space=pltpu.VMEM)
    anywhere = pl.BlockSpec(memory_space=pl.ANY)
    results = pl.pallas_call(
        functools.partial(whole_kernel, [len(group) for group in groups]),
        out_shape=(
            jax.ShapeDtypeStruct(object_field.shape, jnp.float32),
            jax.ShapeDtypeStruct(probe_field.shape, jnp.float32),
        ),
        in_specs=[smem, smem, anywhere, anywhere, anywhere, anywhere],
        out_specs=(vmem, vmem),
        scratch_shapes=sum(groups, []),
        compiler_params=pltpu.CompilerParams(
            collective_id=0, has_side_effects=True, vmem_limit_bytes=60 * 2**20
        ),
        name="refinement",
    )(offsets, counts, object_field, probe_field, amplitudes, tables)
    return hand_over(*results)


def shards(object_field, probe_field, amplitudes, offsets, counts):
    tile_rows = object_field.shape[1]
    tile_cols = object_field.shape[2]
    window = probe_field.shape[1]
    margin = HALO
    tables = jnp.asarray(make_tables(window))
    current = object_field
    probe_now = probe_field
    for outer_step in range(OUTER):
        probe_mean = jnp.sum(probe_now * probe_now) / (window * window)
        lower_rows = shifted(current[:, :margin, :], "row", -1)
        taller = jnp.concatenate([current, lower_rows], axis=1)
        right_cols = shifted(taller[:, :, :margin], "col", -1)
        extended = jnp.concatenate([taller, right_cols], axis=2)
        grad_ext, probe_grad, power = one_pass(
            extended, probe_now, amplitudes, offsets, counts, tables
        )
        rim_right = shifted(grad_ext[:, :, tile_cols:], "col", 1)
        narrowed = grad_ext[:, :, :tile_cols]
        narrowed = jnp.concatenate(
            [narrowed[:, :, :margin] + rim_right, narrowed[:, :, margin:]], axis=2
        )
        rim_lower = shifted(narrowed[:, tile_rows:, :], "row", 1)
        tile_grad = jnp.concatenate(
            [narrowed[:, :margin, :] + rim_lower, narrowed[:, margin:tile_rows, :]], axis=1
        )
        current = current + object_step * tile_grad / (probe_mean + tiny_value)
        power_old = jnp.sum(probe_now * probe_now)
        summed_grad, summed_power = lax.psum((probe_grad, power[0]), ("row", "col"))
        moved_probe = probe_now + summed_grad / (
            jnp.sum(summed_power) / (window * window) + tiny_value
        )
        power_new = jnp.sum(moved_probe * moved_probe)
        probe_now = moved_probe * jnp.sqrt(power_old / (power_new + tiny_value))
    return (current, probe_now)


def solution(mesh):
    rows, cols = mesh.shape["row"], mesh.shape["col"]

    def shards_here(*args):
        deep = Sums.chunk(rows, cols, args[1].shape[1])
        return (shards_by_kernel if deep and deep % 8 == 0 else shards)(*args)

    return jax.shard_map(
        shards_here,
        mesh=mesh,
        in_specs=(
            P(None, "row", "col"),
            P(),
            P("row", "col", None),
            P("row", "col", None, None),
            P("row", "col"),
        ),
        out_specs=(P(None, "row", "col"), P()),
        check_vma=False,
    )
```
